256 devices in a mesh: occ: 32 (over x, z_hi, y), grp: 8 (over z_lo, core).
Axes of the slice: x: 4, y: 4, z: 8 (z_hi: 2, z_lo: 4; z = z_hi * 4 + z_lo), core: 2. Of those that a mesh axis runs over, the one named last changes fastest.
Arguments:
- b_factors: bfloat16 [256, 512, 768], P(('occ', 'grp')), may hold values from -0.29882812 to 0.29882812
- occ_energy: float32 [256], replicated, may hold values from -2 to -0.5
- vir_energy: float32 [512], replicated, may hold values from 0.2 to 3
- integrals: bfloat16 [512, 768, 1024], P('grp', 'occ'), may hold values from -0.0625 to 0.0625
- window_start: int32 [1], replicated, may hold values from 0 to 31
Outputs:
- aux_metric: float32 [768, 768], P('occ', 'grp')
- lagrangian: float32 [256, 1024], P('occ', 'grp')
The draws below stay inside these ranges and needn't reach their ends.
Inputs may be any that keep to these rules, and one draw needn't show every extreme that they name: `window_start`: the cycle offset of the window's first pair.
All inputs are finite; a program needn't handle non-finite values.
Results may differ from the reference program's by a relative error of at most 0.0034.
Values may be sent and summed in bfloat16 or wider, within the bound.
No kernel may reach another device: no remote copies, remote signals or barrier semaphores. Data moves between devices by JAX's collectives and lax.ppermute only.
A program may use at most 64 MiB of HBM per device.

```python
import math
import jax
import jax.numpy as jnp
from jax import lax

V = 512
NAUX = 768
NORB = 1024
SHIFTS = 3
O = 256
N_OCC = 32
N_GRP = 8


def steps_of(stream_key, dims, pieces, smallest, top_value):
    def one(position, shards_of):
        steps = jax.random.uniform(jax.random.fold_in(jax.random.fold_in(stream_key, 6), position), (shards_of,), jnp.float32, smallest / len(pieces), top_value / len(pieces))
        return jnp.repeat(jnp.exp(steps), dims[position] // shards_of).reshape((-1,) + (1,) * (len(dims) - position - 1))

    gain = one(*pieces[0])
    for cut in pieces[1:]:
        gain = gain * one(*cut)
    return gain


def noise(rng, shape, spread, reach, cuts=(), held_as=jnp.bfloat16):
    values = spread * jax.random.normal(rng, shape, jnp.float32)
    if cuts:
        values = values * steps_of(rng, shape, cuts, -0.22, 0.18)
    return jnp.clip(values, -reach, reach).astype(held_as)


def setup_inputs(seed: int = 0) -> dict:
    arg_keys = jax.random.split(jax.random.key(seed), 6)
    b_factors = noise(arg_keys[0], (O, V, NAUX), 0.05, 0.29882812, ((0, 256),))
    occ_energy = jnp.clip(jax.random.uniform(arg_keys[1], (O,), jnp.float32, -2.0, -0.5), -2.0, -0.5)
    vir_energy = jnp.clip(jnp.exp(jax.random.uniform(arg_keys[2], (V,), jnp.float32, math.log(0.2), math.log(3.0))), 0.2, 3.0)
    integrals = noise(arg_keys[3], (V, NAUX, NORB), (V * NAUX // 50) ** -0.5, 0.0625, ((0, 8), (1, 32)))
    window_start = jax.random.randint(arg_keys[4], (1,), 0, N_OCC).astype(jnp.int32)
    return {"b_factors": b_factors, "occ_energy": occ_energy, "vir_energy": vir_energy, "integrals": integrals, "window_start": window_start}


def reference(b_factors, occ_energy, vir_energy, integrals, window_start):
    offset = window_start[0]

    def per_orbital(orbital):
        cycle_pos = orbital // N_GRP
        group_pos = orbital % N_GRP
        own_rows = b_factors[orbital]
        total = jnp.zeros((V, NAUX), jnp.float32)
        for step_no in range(SHIFTS):
            partner = (jnp.mod(cycle_pos - offset - step_no, N_OCC) * N_GRP + group_pos).astype(jnp.int32)
            other_rows = lax.dynamic_index_in_dim(b_factors, partner, 0, keepdims=False)
            intersection = lax.dot_general(own_rows, other_rows, (((1,), (1,)), ((), ())), preferred_element_type=jnp.float32)
            denominator = occ_energy[orbital] + occ_energy[partner] - vir_energy[:, None] - vir_energy[None, :]
            amplitude = intersection / denominator
            combined = (2.0 * amplitude - amplitude.T).astype(jnp.bfloat16)
            total = total + jnp.dot(combined, other_rows, preferred_element_type=jnp.float32)
        return total.astype(jnp.bfloat16)

    density = lax.map(per_orbital, jnp.arange(O, dtype=jnp.int32))
    flat_density = density.reshape(O * V, NAUX)
    aux_metric = jnp.dot(flat_density.T, b_factors.reshape(O * V, NAUX), preferred_element_type=jnp.float32)
    lagrangian = jnp.dot(density.reshape(O, V * NAUX), integrals.reshape(V * NAUX, NORB), preferred_element_type=jnp.float32)
    return aux_metric, lagrangian
```

```python
import jax
import jax.numpy as jnp
from jax import lax
from jax.sharding import Mesh, PartitionSpec as P

BF16 = jnp.bfloat16
F32 = jnp.float32


def exchange_all(x, axes):
    return lax.all_to_all(x, axes, split_axis=0, concat_axis=0, tiled=True)


def swap_cores(x):
    return lax.ppermute(x, "core", [(0, 1), (1, 0)])


def local(b_factors, occ_energy, vir_energy, integrals, window_start):
    n_cyc = lax.axis_size("occ")
    n_zl = lax.axis_size("zl")
    cyc = lax.axis_index("occ")
    core = lax.axis_index("core")
    grp = lax.axis_index("zl") * 2 + core
    n_grp = n_zl * 2
    own = b_factors[0]
    n_vir, n_aux = own.shape
    shift = jnp.mod(window_start[0] + 1, n_cyc)

    ring = [(i, (i + 1) % n_cyc) for i in range(n_cyc)]
    prev_rows = lax.ppermute(own, "occ", ring)
    next_rows = lax.ppermute(own, "occ", [(b, a) for a, b in ring])

    ints = jnp.transpose(integrals, (1, 0, 2))
    other_ints = swap_cores(ints)
    first = jnp.where(core == 0, ints, other_ints)
    second = jnp.where(core == 0, other_ints, ints)
    chip_ints = jnp.concatenate([first, second], axis=1)

    spread = exchange_all(own.reshape(n_cyc, n_vir // n_cyc, n_aux), "occ")
    turned = lax.dynamic_slice_in_dim(jnp.concatenate([spread, spread], axis=0), shift, n_cyc, axis=0)
    rows_i = exchange_all(turned, "occ").reshape(n_vir, n_aux)

    i_cyc = jnp.mod(cyc + shift, n_cyc)
    energy_i = occ_energy[i_cyc * n_grp + grp]
    vir_sum = vir_energy[:, None] + vir_energy[None, :]

    total = jnp.zeros((n_aux, n_vir), F32)
    for delta, rows_j in ((0, own), (1, next_rows), (-1, prev_rows)):
        energy_j = occ_energy[jnp.mod(cyc + delta, n_cyc) * n_grp + grp]
        inter = lax.dot_general(rows_i, rows_j, (((1,), (1,)), ((), ())), preferred_element_type=F32)
        inter_t = lax.dot_general(rows_j, rows_i, (((1,), (1,)), ((), ())), preferred_element_type=F32)
        combined_t = ((2.0 * inter_t - inter) / (energy_i + energy_j - vir_sum)).astype(BF16)
        total = total + lax.dot_general(
            rows_j, combined_t, (((0,), (0,)), ((), ())), preferred_element_type=F32
        )
    density_t = total.astype(BF16)

    aux_blk = n_aux // n_cyc
    chip_vir = n_vir // n_zl
    moved = exchange_all(
        density_t.reshape(n_cyc, aux_blk, n_zl, chip_vir).transpose(0, 2, 1, 3).reshape(n_cyc * n_zl, aux_blk, chip_vir),
        ("occ", "zl"),
    )

    col_blk = n_aux // n_grp
    cols = rows_i.reshape(n_vir, n_zl, 2, col_blk)
    even = jnp.pad(cols[:, :, 0], ((0, 0), (0, 0), (0, 128 - col_blk))).reshape(n_vir, n_zl * 128)
    odd = jnp.pad(cols[:, :, 1], ((0, 0), (0, 0), (0, 128 - col_blk))).reshape(n_vir, n_zl * 128)
    keep_cols = jnp.where(core == 0, even, odd)
    send_cols = jnp.where(core == 0, odd, even)
    aux_send = jnp.dot(density_t, send_cols, preferred_element_type=F32).astype(BF16)
    aux_keep = jnp.dot(density_t, keep_cols, preferred_element_type=F32)
    aux_chip = (aux_keep + swap_cores(aux_send).astype(F32)).astype(BF16)
    aux_parts = aux_chip.reshape(n_cyc, aux_blk, n_zl, 128).transpose(0, 2, 1, 3)

    lag = lax.dot_general(moved, chip_ints, (((1, 2), (0, 1)), ((), ())), preferred_element_type=F32).astype(BF16)
    orb_blk = lag.shape[1] // n_grp
    lag = lag.reshape(n_cyc, n_zl, n_zl, 2, orb_blk).transpose(0, 2, 1, 3, 4)
    lag_keep = jnp.where(core == 0, lag[:, :, :, 0], lag[:, :, :, 1])
    lag_send = jnp.where(core == 0, lag[:, :, :, 1], lag[:, :, :, 0])
    lag_parts = jnp.concatenate([lag_keep, swap_cores(lag_send)], axis=2)
    lag_parts = lax.dynamic_slice_in_dim(
        jnp.concatenate([lag_parts, lag_parts], axis=0), jnp.mod(-shift, n_cyc), n_cyc, axis=0
    )

    parts = jnp.concatenate([lag_parts, aux_parts], axis=2).reshape(n_cyc * n_zl, 2 * n_zl + aux_blk, 128)
    sums = jnp.sum(exchange_all(parts, ("occ", "zl")).astype(F32), axis=0)
    aux_metric = sums[2 * n_zl :, :col_blk]
    same, cross = sums[:n_zl], sums[n_zl : 2 * n_zl]
    low = jnp.where(core == 0, same, cross)
    high = jnp.where(core == 0, cross, same)
    lagrangian = jnp.stack([low, high], axis=1).reshape(2 * n_zl, orb_blk)
    return (aux_metric, lagrangian)


def solution(mesh):
    n_occ, n_grp = mesh.shape["occ"], mesh.shape["grp"]
    fine = Mesh(mesh.devices.reshape(n_occ, n_grp // 2, 2), ("occ", "zl", "core"))
    grp = ("zl", "core")
    placed = (P(("occ", "zl", "core"), None, None), P(), P(), P(grp, "occ", None), P())
    return jax.shard_map(
        local,
        mesh=fine,
        in_specs=placed,
        out_specs=(P("occ", grp), P("occ", grp)),
        check_vma=False,
    )
```

```python
import jax
import jax.numpy as jnp
from jax import lax
from jax.experimental import pallas as pl
from jax.experimental.pallas import tpu as pltpu
from jax.sharding import Mesh, PartitionSpec as P

BF16 = jnp.bfloat16
F32 = jnp.float32
LANES = 128
VMEM_BYTES = 40 * 1024 * 1024
CYC = ("oh", "yl")
DEST = ("oh", "zl")

vmem = pl.BlockSpec(memory_space=pltpu.VMEM)
smem = pl.BlockSpec(memory_space=pltpu.SMEM)


def exchange_all(x, axes):
    return lax.all_to_all(x, axes, split_axis=0, concat_axis=0, tiled=True)


def swap_cores(x):
    return lax.ppermute(x, "core", [(0, 1), (1, 0)])


def swap_yl(x):
    return lax.ppermute(x, "yl", [(0, 1), (1, 0)])


def swap_both(x):
    return lax.ppermute(x, ("yl", "core"), [(i, 3 - i) for i in range(4)])


def dot(a, b, ca, cb):
    return lax.dot_general(a, b, (((ca,), (cb,)), ((), ())), preferred_element_type=F32)


def call(kernel, outs, scratch, flops, nbytes, *args, specs):
    return pl.pallas_call(
        kernel,
        out_shape=outs,
        in_specs=specs,
        out_specs=jax.tree.map(lambda _: vmem, outs),
        scratch_shapes=scratch,
        compiler_params=pltpu.CompilerParams(vmem_limit_bytes=VMEM_BYTES),
        cost_estimate=pl.CostEstimate(flops=flops, bytes_accessed=nbytes, transcendentals=0),
    )(*args)


def pair_kernel(energy, vir_row, vir_col, rows_i, own, nxt, prv, out):
    n_cyc, n_h, aux_blk, lanes = out.shape
    n_vir, n_aux = rows_i.shape
    blk = 2 * lanes

    def body(step, carry):
        start = pl.multiple_of(step * blk, blk)
        block_i = rows_i[pl.ds(start, blk), :]
        vir_sum = vir_col[pl.ds(start, blk), :] + vir_row[...]
        total = jnp.zeros((blk, n_aux), F32)
        for t, rows_j in enumerate((own, nxt, prv)):
            inter = dot(block_i, rows_j[...], 1, 1)
            inter_t = dot(rows_j[pl.ds(start, blk), :], rows_i[...], 1, 1)
            combined = ((2.0 * inter - inter_t) / (energy[t] - vir_sum)).astype(BF16)
            total = total + dot(combined, rows_j[...], 1, 0)
        for half in range(2):
            turned = jnp.transpose(total[half * lanes : (half + 1) * lanes])
            out[:, step * 2 + half] = turned.reshape(n_cyc, aux_blk, lanes).astype(BF16)
        return carry

    lax.fori_loop(0, n_h // 2, body, 0)


def aux_kernel(place, dens, rows_i, keep, send, acc):
    n_cyc, n_h, aux_blk, lanes = dens.shape
    n_vir, n_aux = rows_i.shape
    n_grp = 2 * n_h
    col_blk = n_aux // n_grp
    yl, core = place[1], place[2]
    pad = jnp.zeros((lanes, lanes - col_blk), BF16)
    for h in range(n_h):
        block = rows_i[h * lanes : (h + 1) * lanes, :]
        pieces = []
        for g in range(n_grp):
            pieces += [block[:, g * col_blk : (g + 1) * col_blk], pad]
        left = dens[:, h].reshape(n_cyc * aux_blk, lanes)
        term = dot(left, jnp.concatenate(pieces, axis=1), 1, 0)
        if h == 0:
            acc[...] = term
        else:
            acc[...] += term

    def body(oh, carry):
        for other in range(2):
            row = pl.multiple_of((2 * oh + jnp.bitwise_xor(yl, other)) * aux_blk, 8)
            for g in range(n_grp):
                value = acc[pl.ds(row, aux_blk), g * lanes : (g + 1) * lanes]
                cross = jnp.bitwise_xor(core, g % 2)
                slot = other * 2 + cross
                send[slot, oh * n_h + g // 2] = value.astype(BF16)
                if other == 0:

                    @pl.when(cross == 0)
                    def _():
                        keep[oh * n_h + g // 2] = value

        return carry

    lax.fori_loop(0, n_cyc // 2, body, 0)


def lag_kernel(place, moved, ints, other_ints, parts, wide, acc):
    n_src, aux_blk, lanes = moved.shape
    n_orb = ints.shape[2]
    n_dest = parts.shape[1]
    n_zl = parts.shape[2]
    n_cyc = n_src // n_zl
    shift, yl, core = place[0], place[1], place[2]
    wide[...] = moved[...].reshape(n_src * aux_blk, lanes).astype(F32)
    for p in range(0, aux_blk, 2):
        left, right = [], []
        for q in (p, p + 1):
            x = wide[pl.ds(q, n_src, stride=aux_blk), :]
            left.append(pltpu.roll(x, core * (lanes // 2), 1).astype(BF16))
            right += [ints[q], other_ints[q]]
        term = dot(jnp.concatenate(left, axis=1), jnp.concatenate(right, axis=0), 1, 0)
        if p == 0:
            acc[...] = term
        else:
            acc[...] += term
    for k in range(n_cyc):
        target = lax.rem(k + shift, n_cyc)
        other = jnp.bitwise_xor(jnp.bitwise_and(target, 1), yl)
        for g in range(n_orb // lanes):
            slot = other * 2 + jnp.bitwise_xor(core, g % 2)
            parts[slot, lax.div(target, 2) * n_zl + g // 2] = acc[
                k * n_zl : (k + 1) * n_zl, g * lanes : (g + 1) * lanes
            ]


def join_kernel(lag_keep, lag_c, lag_y, lag_yc, aux_keep, aux_c, aux_y, aux_yc, out):
    lag = jnp.concatenate([lag_keep[...] + lag_y[...], lag_c[...] + lag_yc[...]], axis=1)
    aux = aux_keep[...] + aux_c[...].astype(F32) + aux_y[...].astype(F32) + aux_yc[...].astype(F32)
    out[...] = jnp.concatenate([lag, aux], axis=1).astype(BF16)


def local(b_factors, occ_energy, vir_energy, integrals, window_start):
    n_cyc = lax.axis_size("oh") * 2
    n_zl = lax.axis_size("zl")
    n_grp = n_zl * 2
    yl = lax.axis_index("yl")
    core = lax.axis_index("core")
    cyc = lax.axis_index("oh") * 2 + yl
    grp = lax.axis_index("zl") * 2 + core
    own = b_factors[0]
    n_vir, n_aux = own.shape
    n_orb = integrals.shape[2]
    aux_blk = n_aux // n_cyc
    col_blk = n_aux // n_grp
    shift = jnp.mod(window_start[0] + 1, n_cyc)
    place = jnp.stack([shift, yl, core]).astype(jnp.int32)

    ring = [(i, (i + 1) % n_cyc) for i in range(n_cyc)]
    prev_rows = lax.ppermute(own, CYC, ring)
    next_rows = lax.ppermute(own, CYC, [(b, a) for a, b in ring])

    ints = jnp.transpose(integrals, (1, 0, 2))
    other_ints = swap_cores(ints)

    spread = exchange_all(own.reshape(n_cyc, n_vir // n_cyc, n_aux), CYC)
    turned = lax.dynamic_slice_in_dim(jnp.concatenate([spread, spread], axis=0), shift, n_cyc, axis=0)
    rows_i = exchange_all(turned, CYC).reshape(n_vir, n_aux)

    energy_i = occ_energy[jnp.mod(cyc + shift, n_cyc) * n_grp + grp]
    energy_j = occ_energy[jnp.mod(cyc + jnp.array([0, 1, -1]), n_cyc) * n_grp + grp]
    dens = call(
        pair_kernel,
        jax.ShapeDtypeStruct((n_cyc, n_vir // LANES, aux_blk, LANES), BF16),
        [],
        18 * n_vir * n_vir * n_aux,
        5 * 2 * n_vir * n_aux,
        energy_i + energy_j,
        vir_energy[None, :],
        vir_energy[:, None],
        rows_i,
        own,
        next_rows,
        prev_rows,
        specs=[smem] + [vmem] * 6,
    )
    n_dest = n_cyc // 2 * n_zl
    moved = exchange_all(dens.reshape(n_cyc * n_zl, aux_blk, LANES), CYC + ("zl",))

    aux_keep, aux_send = call(
        aux_kernel,
        (
            jax.ShapeDtypeStruct((n_dest, aux_blk, LANES), F32),
            jax.ShapeDtypeStruct((4, n_dest, aux_blk, LANES), BF16),
        ),
        [pltpu.VMEM((n_aux, n_grp * LANES), F32)],
        2 * n_vir * n_aux * n_aux,
        10 * n_vir * n_aux,
        place,
        dens,
        rows_i,
        specs=[smem, vmem, vmem],
    )
    aux_c, aux_y, aux_yc = swap_cores(aux_send[1]), swap_yl(aux_send[2]), swap_both(aux_send[3])

    lag = call(
        lag_kernel,
        jax.ShapeDtypeStruct((4, n_dest, n_zl, LANES), F32),
        [pltpu.VMEM((n_vir * n_aux // LANES, LANES), F32), pltpu.VMEM((n_cyc * n_zl, n_orb), F32)],
        2 * n_vir * n_aux * n_orb,
        2 * n_vir * n_aux * 10,
        place,
        moved,
        ints,
        other_ints,
        specs=[smem] + [vmem] * 3,
    )
    lag_c, lag_y, lag_yc = swap_cores(lag[1]), swap_yl(lag[2]), swap_both(lag[3])
    parts = call(
        join_kernel,
        jax.ShapeDtypeStruct((n_dest, 2 * n_zl + aux_blk, LANES), BF16),
        [],
        10 * n_dest * 32 * LANES,
        20 * n_dest * 32 * LANES,
        lag[0],
        lag_c,
        lag_y,
        lag_yc,
        aux_keep,
        aux_c,
        aux_y,
        aux_yc,
        specs=[vmem] * 8,
    )
    sums = jnp.sum(exchange_all(parts, DEST).astype(F32), axis=0)
    aux_metric = sums[2 * n_zl :, :col_blk]
    same, cross = sums[:n_zl], sums[n_zl : 2 * n_zl]
    low = jnp.where(core == 0, same, cross)
    high = jnp.where(core == 0, cross, same)
    lagrangian = jnp.stack([low, high], axis=1).reshape(n_grp, LANES)
    return (aux_metric, lagrangian)


def solution(mesh):
    n_occ, n_grp = mesh.shape["occ"], mesh.shape["grp"]
    fine = Mesh(mesh.devices.reshape(n_occ // 2, 2, n_grp // 2, 2), ("oh", "yl", "zl", "core"))
    grp = ("zl", "core")
    placed = (P(CYC + grp, None, None), P(), P(), P(grp, CYC, None), P())
    return jax.shard_map(
        local,
        mesh=fine,
        in_specs=placed,
        out_specs=(P(CYC, grp), P(CYC, grp)),
        check_vma=False,
    )
```

```python
import jax
import jax.numpy as jnp
from jax import lax
from jax.experimental import pallas as pl
from jax.experimental.pallas import tpu as pltpu
from jax.sharding import Mesh, PartitionSpec as P

BF16 = jnp.bfloat16
F32 = jnp.float32
LANES = 128
VMEM_BYTES = 40 * 1024 * 1024
CYC = ("oh", "yl")
DEST = ("oh", "zl")

vmem = pl.BlockSpec(memory_space=pltpu.VMEM)
smem = pl.BlockSpec(memory_space=pltpu.SMEM)


def exchange_all(x, axes):
    return lax.all_to_all(x, axes, split_axis=0, concat_axis=0, tiled=True)


def swap_cores(x):
    return lax.ppermute(x, "core", [(0, 1), (1, 0)])


def swap_yl(x):
    return lax.ppermute(x, "yl", [(0, 1), (1, 0)])


def swap_both(x):
    return lax.ppermute(x, ("yl", "core"), [(i, 3 - i) for i in range(4)])


def dot(a, b, ca, cb):
    return lax.dot_general(a, b, (((ca,), (cb,)), ((), ())), preferred_element_type=F32)


def call(kernel, outs, scratch, flops, nbytes, *args, specs):
    return pl.pallas_call(
        kernel,
        out_shape=outs,
        in_specs=specs,
        out_specs=jax.tree.map(lambda _: vmem, outs),
        scratch_shapes=scratch,
        compiler_params=pltpu.CompilerParams(vmem_limit_bytes=VMEM_BYTES),
        cost_estimate=pl.CostEstimate(flops=flops, bytes_accessed=nbytes, transcendentals=0),
    )(*args)


def turn_kernel(place, spread, out):
    n_cyc = spread.shape[0]
    shift = place[0]

    def body(pair, carry):
        for odd in range(2):
            d = 2 * pair + odd
            out[d, 0] = spread[lax.rem(d + shift, n_cyc)]
            out[d, 1] = spread[lax.rem(d + (2 * odd - 1) + n_cyc, n_cyc)]
        return carry

    lax.fori_loop(0, n_cyc // 2, body, 0)


def pair_kernel(energy, vir_row, vir_col, rows, own, mate, out):
    n_cyc, n_h, aux_blk, lanes = out.shape
    n_vir, n_aux = own.shape
    sub = rows.shape[2]
    blk = 2 * lanes
    rows_i = rows[:, 0].reshape(n_vir, n_aux)
    far = rows[:, 1].reshape(n_vir, n_aux)

    def body(step, carry):
        start = pl.multiple_of(step * blk, blk)
        chunk = pl.ds(step * (blk // sub), blk // sub)
        block_i = rows[chunk, 0].reshape(blk, n_aux)
        block_far = rows[chunk, 1].reshape(blk, n_aux)
        vir_sum = vir_col[pl.ds(start, blk), :] + vir_row[...]
        total = jnp.zeros((blk, n_aux), F32)
        for t, (block_j, rows_j) in enumerate(
            ((own[pl.ds(start, blk), :], own[...]), (mate[pl.ds(start, blk), :], mate[...]), (block_far, far))
        ):
            inter = dot(block_i, rows_j, 1, 1)
            inter_t = dot(block_j, rows_i, 1, 1)
            combined = ((2.0 * inter - inter_t) / (energy[t] - vir_sum)).astype(BF16)
            total = total + dot(combined, rows_j, 1, 0)
        for half in range(2):
            turned = jnp.transpose(total[half * lanes : (half + 1) * lanes])
            out[:, step * 2 + half] = turned.reshape(n_cyc, aux_blk, lanes).astype(BF16)
        return carry

    lax.fori_loop(0, n_h // 2, body, 0)


def aux_kernel(place, dens, rows, keep, send, acc):
    n_cyc, n_h, aux_blk, lanes = dens.shape
    sub, n_aux = rows.shape[2:]
    per = lanes // sub
    n_grp = 2 * n_h
    col_blk = n_aux // n_grp
    yl, core = place[1], place[2]
    pad = jnp.zeros((lanes, lanes - col_blk), BF16)
    for h in range(n_h):
        block = rows[h * per : (h + 1) * per, 0].reshape(lanes, n_aux)
        pieces = []
        for g in range(n_grp):
            pieces += [block[:, g * col_blk : (g + 1) * col_blk], pad]
        left = dens[:, h].reshape(n_cyc * aux_blk, lanes)
        term = dot(left, jnp.concatenate(pieces, axis=1), 1, 0)
        if h == 0:
            acc[...] = term
        else:
            acc[...] += term

    def body(oh, carry):
        for other in range(2):
            row = pl.multiple_of((2 * oh + jnp.bitwise_xor(yl, other)) * aux_blk, 8)
            for g in range(n_grp):
                value = acc[pl.ds(row, aux_blk), g * lanes : (g + 1) * lanes]
                cross = jnp.bitwise_xor(core, g % 2)
                slot = other * 2 + cross
                send[slot, oh * n_h + g // 2] = value.astype(BF16)
                if other == 0:

                    @pl.when(cross == 0)
                    def _():
                        keep[oh * n_h + g // 2] = value

        return carry

    lax.fori_loop(0, n_cyc // 2, body, 0)


def lag_kernel(place, moved, ints, other_ints, parts, wide, acc):
    n_src, aux_blk, lanes = moved.shape
    n_orb = ints.shape[2]
    n_dest = parts.shape[1]
    n_zl = parts.shape[2]
    n_cyc = n_src // n_zl
    shift, yl, core = place[0], place[1], place[2]
    wide[...] = moved[...].reshape(n_src * aux_blk, lanes).astype(F32)
    for p in range(0, aux_blk, 2):
        left, right = [], []
        for q in (p, p + 1):
            x = wide[pl.ds(q, n_src, stride=aux_blk), :]
            left.append(pltpu.roll(x, core * (lanes // 2), 1).astype(BF16))
            right += [ints[q], other_ints[q]]
        term = dot(jnp.concatenate(left, axis=1), jnp.concatenate(right, axis=0), 1, 0)
        if p == 0:
            acc[...] = term
        else:
            acc[...] += term
    for k in range(n_cyc):
        target = lax.rem(k + shift, n_cyc)
        other = jnp.bitwise_xor(jnp.bitwise_and(target, 1), yl)
        for g in range(n_orb // lanes):
            slot = other * 2 + jnp.bitwise_xor(core, g % 2)
            parts[slot, lax.div(target, 2) * n_zl + g // 2] = acc[
                k * n_zl : (k + 1) * n_zl, g * lanes : (g + 1) * lanes
            ]


def join_kernel(lag_keep, lag_c, lag_y, lag_yc, aux_keep, aux_c, aux_y, aux_yc, out):
    lag = jnp.concatenate([lag_keep[...] + lag_y[...], lag_c[...] + lag_yc[...]], axis=1)
    aux = aux_keep[...] + aux_c[...].astype(F32) + aux_y[...].astype(F32) + aux_yc[...].astype(F32)
    out[...] = jnp.concatenate([lag, aux], axis=1).astype(BF16)


def local(b_factors, occ_energy, vir_energy, integrals, window_start):
    n_cyc = lax.axis_size("oh") * 2
    n_zl = lax.axis_size("zl")
    n_grp = n_zl * 2
    yl = lax.axis_index("yl")
    core = lax.axis_index("core")
    cyc = lax.axis_index("oh") * 2 + yl
    grp = lax.axis_index("zl") * 2 + core
    own = b_factors[0]
    n_vir, n_aux = own.shape
    n_orb = integrals.shape[2]
    aux_blk = n_aux // n_cyc
    col_blk = n_aux // n_grp
    shift = jnp.mod(window_start[0] + 1, n_cyc)
    place = jnp.stack([shift, yl, core]).astype(jnp.int32)

    mate = swap_yl(own)

    ints = jnp.transpose(integrals, (1, 0, 2))
    other_ints = swap_cores(ints)

    sub = n_vir // n_cyc
    spread = exchange_all(own.reshape(n_cyc, sub, n_aux), CYC)
    turned = call(
        turn_kernel,
        jax.ShapeDtypeStruct((n_cyc, 2, sub, n_aux), BF16),
        [],
        0,
        8 * n_vir * n_aux,
        place,
        spread,
        specs=[smem, vmem],
    )
    rows = exchange_all(turned, CYC)

    step = 1 - 2 * yl
    energy_i = occ_energy[jnp.mod(cyc + shift, n_cyc) * n_grp + grp]
    energy_j = occ_energy[jnp.mod(cyc + jnp.stack([0, step, -step]), n_cyc) * n_grp + grp]
    dens = call(
        pair_kernel,
        jax.ShapeDtypeStruct((n_cyc, n_vir // LANES, aux_blk, LANES), BF16),
        [],
        18 * n_vir * n_vir * n_aux,
        5 * 2 * n_vir * n_aux,
        energy_i + energy_j,
        vir_energy[None, :],
        vir_energy[:, None],
        rows,
        own,
        mate,
        specs=[smem] + [vmem] * 5,
    )
    n_dest = n_cyc // 2 * n_zl
    moved = exchange_all(dens.reshape(n_cyc * n_zl, aux_blk, LANES), CYC + ("zl",))

    aux_keep, aux_send = call(
        aux_kernel,
        (
            jax.ShapeDtypeStruct((n_dest, aux_blk, LANES), F32),
            jax.ShapeDtypeStruct((4, n_dest, aux_blk, LANES), BF16),
        ),
        [pltpu.VMEM((n_aux, n_grp * LANES), F32)],
        2 * n_vir * n_aux * n_aux,
        10 * n_vir * n_aux,
        place,
        dens,
        rows,
        specs=[smem, vmem, vmem],
    )
    aux_c, aux_y, aux_yc = swap_cores(aux_send[1]), swap_yl(aux_send[2]), swap_both(aux_send[3])

    lag = call(
        lag_kernel,
        jax.ShapeDtypeStruct((4, n_dest, n_zl, LANES), F32),
        [pltpu.VMEM((n_vir * n_aux // LANES, LANES), F32), pltpu.VMEM((n_cyc * n_zl, n_orb), F32)],
        2 * n_vir * n_aux * n_orb,
        2 * n_vir * n_aux * 10,
        place,
        moved,
        ints,
        other_ints,
        specs=[smem] + [vmem] * 3,
    )
    lag_c, lag_y, lag_yc = swap_cores(lag[1]), swap_yl(lag[2]), swap_both(lag[3])
    parts = call(
        join_kernel,
        jax.ShapeDtypeStruct((n_dest, 2 * n_zl + aux_blk, LANES), BF16),
        [],
        10 * n_dest * 32 * LANES,
        20 * n_dest * 32 * LANES,
        lag[0],
        lag_c,
        lag_y,
        lag_yc,
        aux_keep,
        aux_c,
        aux_y,
        aux_yc,
        specs=[vmem] * 8,
    )
    sums = jnp.sum(exchange_all(parts, DEST).astype(F32), axis=0)
    aux_metric = sums[2 * n_zl :, :col_blk]
    same, cross = sums[:n_zl], sums[n_zl : 2 * n_zl]
    low = jnp.where(core == 0, same, cross)
    high = jnp.where(core == 0, cross, same)
    lagrangian = jnp.stack([low, high], axis=1).reshape(n_grp, LANES)
    return (aux_metric, lagrangian)


def solution(mesh):
    n_occ, n_grp = mesh.shape["occ"], mesh.shape["grp"]
    fine = Mesh(mesh.devices.reshape(n_occ // 2, 2, n_grp // 2, 2), ("oh", "yl", "zl", "core"))
    grp = ("zl", "core")
    placed = (P(CYC + grp, None, None), P(), P(), P(grp, CYC, None), P())
    return jax.shard_map(
        local,
        mesh=fine,
        in_specs=placed,
        out_specs=(P(CYC, grp), P(CYC, grp)),
        check_vma=False,
    )
```

```python
import jax
import jax.numpy as jnp
from jax import lax
from jax.experimental import pallas as pl
from jax.experimental.pallas import tpu as pltpu
from jax.sharding import Mesh, PartitionSpec as P

BF16 = jnp.bfloat16
F32 = jnp.float32
LANES = 128
VMEM_BYTES = 40 * 1024 * 1024
CYC = ("x", "zh", "yh", "yl")
PLANE = ("x", "yh", "yl", "core")
DEPTH = ("zh", "zl")
N_Y = 4

vmem = pl.BlockSpec(memory_space=pltpu.VMEM)
smem = pl.BlockSpec(memory_space=pltpu.SMEM)


def exchange_all(x, axes):
    return lax.all_to_all(x, axes, split_axis=0, concat_axis=0, tiled=True)


def swap_cores(x):
    return lax.ppermute(x, "core", [(0, 1), (1, 0)])


def swap_yl(x):
    return lax.ppermute(x, "yl", [(0, 1), (1, 0)])


def dot(a, b, ca, cb):
    return lax.dot_general(a, b, (((ca,), (cb,)), ((), ())), preferred_element_type=F32)


def call(kernel, outs, scratch, flops, nbytes, *args, specs):
    return pl.pallas_call(
        kernel,
        out_shape=outs,
        in_specs=specs,
        out_specs=jax.tree.map(lambda _: vmem, outs),
        scratch_shapes=scratch,
        compiler_params=pltpu.CompilerParams(vmem_limit_bytes=VMEM_BYTES),
        cost_estimate=pl.CostEstimate(flops=flops, bytes_accessed=nbytes, transcendentals=0),
    )(*args)


def turn_kernel(place, spread, out):
    n_cyc = spread.shape[0]
    shift = place[0]

    def body(pair, carry):
        for odd in range(2):
            d = 2 * pair + odd
            out[d, 0] = spread[lax.rem(d + shift, n_cyc)]
            out[d, 1] = spread[lax.rem(d + (2 * odd - 1) + n_cyc, n_cyc)]
        return carry

    lax.fori_loop(0, n_cyc // 2, body, 0)


def pair_kernel(energy, vir_row, vir_col, rows, own, mate, out):
    n_cyc, n_h, aux_blk, lanes = out.shape
    n_vir, n_aux = own.shape
    sub = rows.shape[2]
    blk = 2 * lanes
    rows_i = rows[:, 0].reshape(n_vir, n_aux)
    far = rows[:, 1].reshape(n_vir, n_aux)

    def body(step, carry):
        start = pl.multiple_of(step * blk, blk)
        chunk = pl.ds(step * (blk // sub), blk // sub)
        block_i = rows[chunk, 0].reshape(blk, n_aux)
        block_far = rows[chunk, 1].reshape(blk, n_aux)
        vir_sum = vir_col[pl.ds(start, blk), :] + vir_row[...]
        total = jnp.zeros((blk, n_aux), F32)
        for t, (block_j, rows_j) in enumerate(
            ((own[pl.ds(start, blk), :], own[...]), (mate[pl.ds(start, blk), :], mate[...]), (block_far, far))
        ):
            inter = dot(block_i, rows_j, 1, 1)
            inter_t = dot(block_j, rows_i, 1, 1)
            combined = ((2.0 * inter - inter_t) / (energy[t] - vir_sum)).astype(BF16)
            total = total + dot(combined, rows_j, 1, 0)
        for half in range(2):
            turned = jnp.transpose(total[half * lanes : (half + 1) * lanes])
            out[:, step * 2 + half] = turned.reshape(n_cyc, aux_blk, lanes).astype(BF16)
        return carry

    lax.fori_loop(0, n_h // 2, body, 0)


def aux_kernel(place, dens, rows, near, far, acc):
    n_cyc, n_h, aux_blk, lanes = dens.shape
    sub, n_aux = rows.shape[2:]
    per = lanes // sub
    n_grp = near.shape[1]
    col_blk = n_aux // n_grp
    core = place[2]
    pad = jnp.zeros((lanes, lanes - col_blk), BF16)
    for h in range(n_h):
        block = rows[h * per : (h + 1) * per, 0].reshape(lanes, n_aux)
        pieces = []
        for g in range(n_grp):
            pieces += [block[:, g * col_blk : (g + 1) * col_blk], pad]
        left = dens[:, h].reshape(n_cyc * aux_blk, lanes)
        term = dot(left, jnp.concatenate(pieces, axis=1), 1, 0)
        if h == 0:
            acc[...] = term
        else:
            acc[...] += term

    def body(xy, carry):
        base = lax.div(xy, N_Y) * (2 * N_Y) + lax.rem(xy, N_Y)
        row = pl.multiple_of((base + N_Y * core) * aux_blk, 8)
        row_far = pl.multiple_of((base + N_Y * (1 - core)) * aux_blk, 8)
        for g in range(n_grp):
            cols = slice(g * lanes, (g + 1) * lanes)
            near[xy, g] = acc[pl.ds(row, aux_blk), cols]
            far[xy, g] = acc[pl.ds(row_far, aux_blk), cols].astype(BF16)
        return carry

    lax.fori_loop(0, n_cyc // 2, body, 0)


def fold_kernel(place, near, far, keep, send):
    n_half = keep.shape[1]
    yl = place[1]
    for g in range(n_half):
        mine = yl * n_half + g
        other = (1 - yl) * n_half + g
        keep[:, g] = near[:, mine] + far[:, mine].astype(F32)
        send[:, g] = (near[:, other] + far[:, other].astype(F32)).astype(BF16)


def lag_kernel(place, moved, ints, other_ints, parts, wide, acc):
    n_src, aux_blk, lanes = moved.shape
    n_orb = ints.shape[2]
    n_zl = parts.shape[2]
    n_cyc = n_src // n_zl
    shift, core = place[0], place[2]
    wide[...] = moved[...].reshape(n_src * aux_blk, lanes).astype(F32)
    for p in range(0, aux_blk, 2):
        left, right = [], []
        for q in (p, p + 1):
            x = wide[pl.ds(q, n_src, stride=aux_blk), :]
            left.append(pltpu.roll(x, core * (lanes // 2), 1).astype(BF16))
            right += [ints[q], other_ints[q]]
        term = dot(jnp.concatenate(left, axis=1), jnp.concatenate(right, axis=0), 1, 0)
        if p == 0:
            acc[...] = term
        else:
            acc[...] += term
    for k in range(n_cyc):
        target = lax.rem(k + shift, n_cyc)
        zh = lax.rem(lax.div(target, N_Y), 2)
        xy = lax.div(target, 2 * N_Y) * N_Y + lax.rem(target, N_Y)
        for g in range(n_orb // lanes):
            parts[xy * 2 + g % 2, zh, g // 2] = acc[k * n_zl : (k + 1) * n_zl, g * lanes : (g + 1) * lanes]


def join_kernel(lag, keep, recv, out):
    n_dest, n_zh, n_zl = lag.shape[:3]
    pieces = [lag[:, a, b] for a in range(n_zh) for b in range(n_zl)]
    n_lag = n_zh * n_zl * lag.shape[3]
    aux_blk, lanes = keep.shape[2:]
    n_low = keep.shape[1] // 2
    out[:, :n_lag] = jnp.concatenate(pieces, axis=1).astype(BF16)
    for xy in range(n_dest // 2):
        for low in range(n_low):
            for c in range(2):
                g = 2 * low + c
                out[2 * xy + c, n_lag + low * aux_blk : n_lag + (low + 1) * aux_blk] = (
                    keep[xy, g] + recv[xy, g].astype(F32)
                ).astype(BF16)


def plane_kernel(got, out):
    n_src = got.shape[0]
    n_z, n_rows, lanes = out.shape
    n_zl = n_z // 2
    n_lag = n_z * n_zl
    aux_blk = n_rows - 2 * n_zl
    n_low = (got.shape[1] - n_lag) // aux_blk
    for c in range(2):
        total = got[c, :n_lag].astype(F32)
        for src in range(c + 2, n_src, 2):
            total = total + got[src, :n_lag].astype(F32)
        for z in range(n_z):
            out[z, c * n_zl : (c + 1) * n_zl] = total[z * n_zl : (z + 1) * n_zl]
        for yl in range(2):
            first = 2 * yl + c
            total = got[first, n_lag:].astype(F32)
            for src in range(first + 4, n_src, 4):
                total = total + got[src, n_lag:].astype(F32)
            for low in range(n_low):
                z = c * n_zl + n_low * yl + low
                out[z, 2 * n_zl :] = total[low * aux_blk : (low + 1) * aux_blk]


def last_kernel(got, aux, lag):
    total = jnp.sum(got[...], axis=0)
    n_zl = lag.shape[0] // 2
    aux[...] = total[2 * n_zl :, : aux.shape[1]]
    for z in range(n_zl):
        for c in range(2):
            lag[2 * z + c : 2 * z + c + 1] = total[c * n_zl + z : c * n_zl + z + 1]


def local(b_factors, occ_energy, vir_energy, integrals, window_start):
    n_cyc = lax.axis_size(CYC)
    n_zl = lax.axis_size("zl")
    n_grp = n_zl * 2
    yl = lax.axis_index("yl")
    core = lax.axis_index("core")
    cyc = lax.axis_index(CYC)
    grp = lax.axis_index("zl") * 2 + core
    own = b_factors[0]
    n_vir, n_aux = own.shape
    n_orb = integrals.shape[2]
    aux_blk = n_aux // n_cyc
    shift = jnp.mod(window_start[0] + 1, n_cyc)
    place = jnp.stack([shift, yl, core]).astype(jnp.int32)

    mate = swap_yl(own)

    ints = jnp.transpose(integrals, (1, 0, 2))
    other_ints = swap_cores(ints)

    sub = n_vir // n_cyc
    spread = exchange_all(own.reshape(n_cyc, sub, n_aux), CYC)
    turned = call(
        turn_kernel,
        jax.ShapeDtypeStruct((n_cyc, 2, sub, n_aux), BF16),
        [],
        0,
        8 * n_vir * n_aux,
        place,
        spread,
        specs=[smem, vmem],
    )
    rows = exchange_all(turned, CYC)

    step = 1 - 2 * yl
    energy_i = occ_energy[jnp.mod(cyc + shift, n_cyc) * n_grp + grp]
    energy_j = occ_energy[jnp.mod(cyc + jnp.stack([0, step, -step]), n_cyc) * n_grp + grp]
    dens = call(
        pair_kernel,
        jax.ShapeDtypeStruct((n_cyc, n_vir // LANES, aux_blk, LANES), BF16),
        [],
        18 * n_vir * n_vir * n_aux,
        5 * 2 * n_vir * n_aux,
        energy_i + energy_j,
        vir_energy[None, :],
        vir_energy[:, None],
        rows,
        own,
        mate,
        specs=[smem] + [vmem] * 5,
    )
    moved = exchange_all(dens.reshape(n_cyc * n_zl, aux_blk, LANES), CYC + ("zl",))

    n_xy = n_cyc // 2
    near, far = call(
        aux_kernel,
        (
            jax.ShapeDtypeStruct((n_xy, n_grp, aux_blk, LANES), F32),
            jax.ShapeDtypeStruct((n_xy, n_grp, aux_blk, LANES), BF16),
        ),
        [pltpu.VMEM((n_aux, n_grp * LANES), F32)],
        2 * n_vir * n_aux * n_aux,
        10 * n_vir * n_aux,
        place,
        dens,
        rows,
        specs=[smem, vmem, vmem],
    )
    keep, send = call(
        fold_kernel,
        (
            jax.ShapeDtypeStruct((n_xy, n_grp // 2, aux_blk, LANES), F32),
            jax.ShapeDtypeStruct((n_xy, n_grp // 2, aux_blk, LANES), BF16),
        ),
        [],
        0,
        9 * n_vir * n_aux,
        place,
        near,
        swap_cores(far),
        specs=[smem, vmem, vmem],
    )
    recv = swap_yl(send)

    lag = call(
        lag_kernel,
        jax.ShapeDtypeStruct((n_cyc, 2, n_zl, n_zl, LANES), F32),
        [pltpu.VMEM((n_vir * n_aux // LANES, LANES), F32), pltpu.VMEM((n_cyc * n_zl, n_orb), F32)],
        2 * n_vir * n_aux * n_orb,
        2 * n_vir * n_aux * 10,
        place,
        moved,
        ints,
        other_ints,
        specs=[smem] + [vmem] * 3,
    )
    n_rows = 2 * n_zl * n_zl + n_zl // 2 * aux_blk
    parts = call(
        join_kernel,
        jax.ShapeDtypeStruct((n_cyc, n_rows, LANES), BF16),
        [],
        0,
        8 * n_cyc * n_rows * LANES,
        lag,
        keep,
        recv,
        specs=[vmem] * 3,
    )
    plane = call(
        plane_kernel,
        jax.ShapeDtypeStruct((2 * n_zl, n_grp + aux_blk, LANES), F32),
        [],
        n_cyc * n_rows * LANES,
        2 * n_cyc * n_rows * LANES,
        exchange_all(parts, PLANE),
        specs=[vmem],
    )
    aux_metric, lagrangian = call(
        last_kernel,
        (jax.ShapeDtypeStruct((aux_blk, n_aux // n_grp), F32), jax.ShapeDtypeStruct((n_grp, LANES), F32)),
        [],
        0,
        4 * 2 * n_zl * 32 * LANES,
        exchange_all(plane, DEPTH),
        specs=[vmem],
    )
    return (aux_metric, lagrangian)


def solution(mesh):
    n_occ, n_grp = mesh.shape["occ"], mesh.shape["grp"]
    sizes = (n_occ // (2 * N_Y), 2, N_Y // 2, 2, n_grp // 2, 2)
    fine = Mesh(mesh.devices.reshape(sizes), CYC + ("zl", "core"))
    grp = ("zl", "core")
    placed = (P(CYC + grp, None, None), P(), P(), P(grp, CYC, None), P())
    return jax.shard_map(
        local,
        mesh=fine,
        in_specs=placed,
        out_specs=(P(CYC, grp), P(CYC, grp)),
        check_vma=False,
    )
```

```python
import jax
import jax.numpy as jnp
from jax import lax
from jax.experimental import pallas as pl
from jax.experimental.pallas import tpu as pltpu
from jax.sharding import Mesh, PartitionSpec as P

BF16 = jnp.bfloat16
F32 = jnp.float32
LANES = 128
VMEM_BYTES = 40 * 1024 * 1024
CYC = ("x", "zh", "yh", "yl")
PLANE = ("x", "yh", "yl", "core")
DEPTH = ("zh", "zl")
N_Y = 4

vmem = pl.BlockSpec(memory_space=pltpu.VMEM)
smem = pl.BlockSpec(memory_space=pltpu.SMEM)


def exchange_all(x, axes):
    return lax.all_to_all(x, axes, split_axis=0, concat_axis=0, tiled=True)


def swap_cores(x):
    return lax.ppermute(x, "core", [(0, 1), (1, 0)])


def swap_yl(x):
    return lax.ppermute(x, "yl", [(0, 1), (1, 0)])


def dot(a, b, ca, cb):
    return lax.dot_general(a, b, (((ca,), (cb,)), ((), ())), preferred_element_type=F32)


def call(kernel, outs, scratch, flops, nbytes, *args, specs):
    return pl.pallas_call(
        kernel,
        out_shape=outs,
        in_specs=specs,
        out_specs=jax.tree.map(lambda _: vmem, outs),
        scratch_shapes=scratch,
        compiler_params=pltpu.CompilerParams(vmem_limit_bytes=VMEM_BYTES),
        cost_estimate=pl.CostEstimate(flops=flops, bytes_accessed=nbytes, transcendentals=0),
    )(*args)


def turn_kernel(place, spread, mate, out):
    del mate
    n_cyc = spread.shape[0]
    shift = place[0]

    def body(pair, carry):
        for odd in range(2):
            d = 2 * pair + odd
            out[d, 0] = spread[lax.rem(d + shift, n_cyc)]
            out[d, 1] = spread[lax.rem(d + (2 * odd - 1) + n_cyc, n_cyc)]
        return carry

    lax.fori_loop(0, n_cyc // 2, body, 0)


def pair_kernel(energy, vir_row, vir_col, rows, own, mate, out):
    n_cyc, n_h, aux_blk, lanes = out.shape
    n_vir, n_aux = own.shape
    sub = rows.shape[2]
    blk = 2 * lanes
    rows_i = rows[:, 0].reshape(n_vir, n_aux)
    far = rows[:, 1].reshape(n_vir, n_aux)

    def body(step, carry):
        start = pl.multiple_of(step * blk, blk)
        chunk = pl.ds(step * (blk // sub), blk // sub)
        block_i = rows[chunk, 0].reshape(blk, n_aux)
        block_far = rows[chunk, 1].reshape(blk, n_aux)
        vir_sum = vir_col[pl.ds(start, blk), :] + vir_row[...]
        total = jnp.zeros((blk, n_aux), F32)
        for t, (block_j, rows_j) in enumerate(
            ((own[pl.ds(start, blk), :], own[...]), (mate[pl.ds(start, blk), :], mate[...]), (block_far, far))
        ):
            inter = dot(block_i, rows_j, 1, 1)
            inter_t = dot(block_j, rows_i, 1, 1)
            combined = ((2.0 * inter - inter_t) / (energy[t] - vir_sum)).astype(BF16)
            total = total + dot(combined, rows_j, 1, 0)
        for half in range(2):
            turned = jnp.transpose(total[half * lanes : (half + 1) * lanes])
            out[:, step * 2 + half] = turned.reshape(n_cyc, aux_blk, lanes).astype(BF16)
        return carry

    lax.fori_loop(0, n_h // 2, body, 0)


def aux_kernel(place, dens, rows, near, far, acc):
    n_cyc, n_h, aux_blk, lanes = dens.shape
    sub, n_aux = rows.shape[2:]
    per = lanes // sub
    n_grp = near.shape[1]
    col_blk = n_aux // n_grp
    core = place[2]
    pad = jnp.zeros((lanes, lanes - col_blk), BF16)
    for h in range(n_h):
        block = rows[h * per : (h + 1) * per, 0].reshape(lanes, n_aux)
        pieces = []
        for g in range(n_grp):
            pieces += [block[:, g * col_blk : (g + 1) * col_blk], pad]
        left = dens[:, h].reshape(n_cyc * aux_blk, lanes)
        term = dot(left, jnp.concatenate(pieces, axis=1), 1, 0)
        if h == 0:
            acc[...] = term
        else:
            acc[...] += term

    def body(xy, carry):
        base = lax.div(xy, N_Y) * (2 * N_Y) + lax.rem(xy, N_Y)
        row = pl.multiple_of((base + N_Y * core) * aux_blk, 8)
        row_far = pl.multiple_of((base + N_Y * (1 - core)) * aux_blk, 8)
        for g in range(n_grp):
            cols = slice(g * lanes, (g + 1) * lanes)
            near[xy, g] = acc[pl.ds(row, aux_blk), cols]
            far[xy, g] = acc[pl.ds(row_far, aux_blk), cols].astype(BF16)
        return carry

    lax.fori_loop(0, n_cyc // 2, body, 0)


def fold_kernel(place, near, far, keep, send):
    n_half = keep.shape[1]
    yl = place[1]
    for g in range(n_half):
        mine = yl * n_half + g
        other = (1 - yl) * n_half + g
        keep[:, g] = near[:, mine] + far[:, mine].astype(F32)
        send[:, g] = (near[:, other] + far[:, other].astype(F32)).astype(BF16)


def lag_kernel(place, moved, ints, other_ints, parts, wide, acc):
    n_src, aux_blk, lanes = moved.shape
    n_orb = ints.shape[2]
    n_zl = parts.shape[2]
    n_cyc = n_src // n_zl
    shift, core = place[0], place[2]
    wide[...] = moved[...].reshape(n_src * aux_blk, lanes).astype(F32)
    for p in range(0, aux_blk, 2):
        left, right = [], []
        for q in (p, p + 1):
            x = wide[pl.ds(q, n_src, stride=aux_blk), :]
            left.append(pltpu.roll(x, core * (lanes // 2), 1).astype(BF16))
            right += [ints[q], other_ints[q]]
        term = dot(jnp.concatenate(left, axis=1), jnp.concatenate(right, axis=0), 1, 0)
        if p == 0:
            acc[...] = term
        else:
            acc[...] += term
    for k in range(n_cyc):
        target = lax.rem(k + shift, n_cyc)
        zh = lax.rem(lax.div(target, N_Y), 2)
        xy = lax.div(target, 2 * N_Y) * N_Y + lax.rem(target, N_Y)
        for g in range(n_orb // lanes):
            parts[xy * 2 + g % 2, zh, g // 2] = acc[k * n_zl : (k + 1) * n_zl, g * lanes : (g + 1) * lanes]


def join_kernel(lag, keep, recv, out):
    n_dest, n_zh, n_zl = lag.shape[:3]
    pieces = [lag[:, a, b] for a in range(n_zh) for b in range(n_zl)]
    n_lag = n_zh * n_zl * lag.shape[3]
    aux_blk, lanes = keep.shape[2:]
    n_low = keep.shape[1] // 2
    out[:, :n_lag] = jnp.concatenate(pieces, axis=1).astype(BF16)
    for xy in range(n_dest // 2):
        for low in range(n_low):
            for c in range(2):
                g = 2 * low + c
                out[2 * xy + c, n_lag + low * aux_blk : n_lag + (low + 1) * aux_blk] = (
                    keep[xy, g] + recv[xy, g].astype(F32)
                ).astype(BF16)


def plane_kernel(got, out):
    n_src = got.shape[0]
    n_z, n_rows, lanes = out.shape
    n_zl = n_z // 2
    n_lag = n_z * n_zl
    aux_blk = n_rows - 2 * n_zl
    n_low = (got.shape[1] - n_lag) // aux_blk
    for c in range(2):
        total = got[c, :n_lag].astype(F32)
        for src in range(c + 2, n_src, 2):
            total = total + got[src, :n_lag].astype(F32)
        for z in range(n_z):
            out[z, c * n_zl : (c + 1) * n_zl] = total[z * n_zl : (z + 1) * n_zl]
        for yl in range(2):
            first = 2 * yl + c
            total = got[first, n_lag:].astype(F32)
            for src in range(first + 4, n_src, 4):
                total = total + got[src, n_lag:].astype(F32)
            for low in range(n_low):
                z = c * n_zl + n_low * yl + low
                out[z, 2 * n_zl :] = total[low * aux_blk : (low + 1) * aux_blk]


def last_kernel(got, aux, lag):
    total = jnp.sum(got[...], axis=0)
    n_zl = lag.shape[0] // 2
    aux[...] = total[2 * n_zl :, : aux.shape[1]]
    for z in range(n_zl):
        for c in range(2):
            lag[2 * z + c : 2 * z + c + 1] = total[c * n_zl + z : c * n_zl + z + 1]


def local(b_factors, occ_energy, vir_energy, integrals, window_start):
    n_cyc = lax.axis_size(CYC)
    n_zl = lax.axis_size("zl")
    n_grp = n_zl * 2
    yl = lax.axis_index("yl")
    core = lax.axis_index("core")
    cyc = lax.axis_index(CYC)
    grp = lax.axis_index("zl") * 2 + core
    own = b_factors[0]
    n_vir, n_aux = own.shape
    n_orb = integrals.shape[2]
    aux_blk = n_aux // n_cyc
    shift = jnp.mod(window_start[0] + 1, n_cyc)
    place = jnp.stack([shift, yl, core]).astype(jnp.int32)

    mate = swap_yl(own)

    ints = jnp.transpose(integrals, (1, 0, 2))
    other_ints = swap_cores(ints)

    sub = n_vir // n_cyc
    spread = exchange_all(own.reshape(n_cyc, sub, n_aux), CYC)
    turned = call(
        turn_kernel,
        jax.ShapeDtypeStruct((n_cyc, 2, sub, n_aux), BF16),
        [],
        0,
        8 * n_vir * n_aux,
        place,
        spread,
        mate,
        specs=[smem, vmem, pl.BlockSpec(memory_space=pl.ANY)],
    )
    rows = exchange_all(turned, CYC)

    step = 1 - 2 * yl
    energy_i = occ_energy[jnp.mod(cyc + shift, n_cyc) * n_grp + grp]
    energy_j = occ_energy[jnp.mod(cyc + jnp.stack([0, step, -step]), n_cyc) * n_grp + grp]
    dens = call(
        pair_kernel,
        jax.ShapeDtypeStruct((n_cyc, n_vir // LANES, aux_blk, LANES), BF16),
        [],
        18 * n_vir * n_vir * n_aux,
        5 * 2 * n_vir * n_aux,
        energy_i + energy_j,
        vir_energy[None, :],
        vir_energy[:, None],
        rows,
        own,
        mate,
        specs=[smem] + [vmem] * 5,
    )
    moved = exchange_all(dens.reshape(n_cyc * n_zl, aux_blk, LANES), CYC + ("zl",))

    n_xy = n_cyc // 2
    near, far = call(
        aux_kernel,
        (
            jax.ShapeDtypeStruct((n_xy, n_grp, aux_blk, LANES), F32),
            jax.ShapeDtypeStruct((n_xy, n_grp, aux_blk, LANES), BF16),
        ),
        [pltpu.VMEM((n_aux, n_grp * LANES), F32)],
        2 * n_vir * n_aux * n_aux,
        10 * n_vir * n_aux,
        place,
        dens,
        rows,
        specs=[smem, vmem, vmem],
    )
    keep, send = call(
        fold_kernel,
        (
            jax.ShapeDtypeStruct((n_xy, n_grp // 2, aux_blk, LANES), F32),
            jax.ShapeDtypeStruct((n_xy, n_grp // 2, aux_blk, LANES), BF16),
        ),
        [],
        0,
        9 * n_vir * n_aux,
        place,
        near,
        swap_cores(far),
        specs=[smem, vmem, vmem],
    )
    recv = swap_yl(send)

    lag = call(
        lag_kernel,
        jax.ShapeDtypeStruct((n_cyc, 2, n_zl, n_zl, LANES), F32),
        [pltpu.VMEM((n_vir * n_aux // LANES, LANES), F32), pltpu.VMEM((n_cyc * n_zl, n_orb), F32)],
        2 * n_vir * n_aux * n_orb,
        2 * n_vir * n_aux * 10,
        place,
        moved,
        ints,
        other_ints,
        specs=[smem] + [vmem] * 3,
    )
    n_rows = 2 * n_zl * n_zl + n_zl // 2 * aux_blk
    parts = call(
        join_kernel,
        jax.ShapeDtypeStruct((n_cyc, n_rows, LANES), BF16),
        [],
        0,
        8 * n_cyc * n_rows * LANES,
        lag,
        keep,
        recv,
        specs=[vmem] * 3,
    )
    plane = call(
        plane_kernel,
        jax.ShapeDtypeStruct((2 * n_zl, n_grp + aux_blk, LANES), F32),
        [],
        n_cyc * n_rows * LANES,
        2 * n_cyc * n_rows * LANES,
        exchange_all(parts, PLANE),
        specs=[vmem],
    )
    aux_metric, lagrangian = call(
        last_kernel,
        (jax.ShapeDtypeStruct((aux_blk, n_aux // n_grp), F32), jax.ShapeDtypeStruct((n_grp, LANES), F32)),
        [],
        0,
        4 * 2 * n_zl * 32 * LANES,
        exchange_all(plane, DEPTH),
        specs=[vmem],
    )
    return (aux_metric, lagrangian)


def solution(mesh):
    n_occ, n_grp = mesh.shape["occ"], mesh.shape["grp"]
    sizes = (n_occ // (2 * N_Y), 2, N_Y // 2, 2, n_grp // 2, 2)
    fine = Mesh(mesh.devices.reshape(sizes), CYC + ("zl", "core"))
    grp = ("zl", "core")
    placed = (P(CYC + grp, None, None), P(), P(), P(grp, CYC, None), P())
    return jax.shard_map(
        local,
        mesh=fine,
        in_specs=placed,
        out_specs=(P(CYC, grp), P(CYC, grp)),
        check_vma=False,
    )
```

```python
import jax
import jax.numpy as jnp
from jax import lax
from jax.experimental import pallas as pl
from jax.experimental.pallas import tpu as pltpu
from jax.sharding import Mesh, PartitionSpec as P

BF16 = jnp.bfloat16
F32 = jnp.float32
LANES = 128
VMEM_BYTES = 40 * 1024 * 1024
PAIR_BYTES = 60 * 1024 * 1024
CYC = ("x", "zh", "yh", "yl")
PLANE = ("x", "yh", "yl", "core")
DEPTH = ("zh", "zl")
N_Y = 4
N_STEP = 2
N_LOAD = 4

vmem = pl.BlockSpec(memory_space=pltpu.VMEM)
smem = pl.BlockSpec(memory_space=pltpu.SMEM)
hbm = pl.BlockSpec(memory_space=pltpu.HBM)


def exchange_all(x, axes):
    return lax.all_to_all(x, axes, split_axis=0, concat_axis=0, tiled=True)


def swap_cores(x):
    return lax.ppermute(x, "core", [(0, 1), (1, 0)])


def swap_yl(x):
    return lax.ppermute(x, "yl", [(0, 1), (1, 0)])


def dot(a, b, ca, cb):
    return lax.dot_general(a, b, (((ca,), (cb,)), ((), ())), preferred_element_type=F32)


def call(kernel, outs, scratch, flops, nbytes, *args, specs, out_spec=vmem, grant=VMEM_BYTES):
    return pl.pallas_call(
        kernel,
        out_shape=outs,
        in_specs=specs,
        out_specs=jax.tree.map(lambda _: out_spec, outs),
        scratch_shapes=scratch,
        compiler_params=pltpu.CompilerParams(vmem_limit_bytes=grant),
        cost_estimate=pl.CostEstimate(flops=flops, bytes_accessed=nbytes, transcendentals=0),
    )(*args)


def turn_kernel(place, spread, out, sems):
    n_pair = spread.shape[0]
    n_cyc = 2 * n_pair
    shift = place[0]
    copies = []

    def copy(src, dst):
        copies.append(pltpu.make_async_copy(src, dst, sems.at[len(copies)]))
        copies[-1].start()

    last = n_pair - 1
    copy(spread.at[pl.ds(1, last), 0], out.at[pl.ds(0, last), 1, 1])
    copy(spread.at[0, 0], out.at[last, 1, 1])
    copy(spread.at[pl.ds(0, last), 1], out.at[pl.ds(1, last), 0, 1])
    copy(spread.at[last, 1], out.at[0, 0, 1])
    for d in range(n_cyc):
        src = lax.rem(d + shift, n_cyc)
        copy(spread.at[lax.div(src, 2), lax.rem(src, 2)], out.at[d // 2, d % 2, 0])
    for c in copies:
        c.wait()


def pair_kernel(energy, vir_row, vir_col, rows_any, own_any, mate_any, out_any, turned, far, own, mate, out, sems):
    n_cyc, n_h, aux_blk, lanes = out.shape
    n_vir, n_aux = own.shape
    sub = turned.shape[1]
    blk = n_vir // N_STEP
    per = blk // lanes
    pairs = ((rows_any.at[:, 0], turned), (own_any, own), (mate_any, mate), (rows_any.at[:, 1], far))
    loads = [pltpu.make_async_copy(src, dst, sems.at[n]) for n, (src, dst) in enumerate(pairs)]
    for load in loads:
        load.start()
    loads[0].wait()
    rows_i = turned[...].reshape(n_vir, n_aux)
    stores = []
    for step in range(N_STEP):
        chunk = slice(step * blk, (step + 1) * blk)
        vir_sum = vir_col[chunk, :] + vir_row[...]
        block_i = rows_i[chunk]
        total = jnp.zeros((blk, n_aux), F32)
        for t in range(3):
            if step == 0:
                loads[t + 1].wait()
            rows_j = (own, mate, far)[t][...].reshape(n_vir, n_aux)
            inter = dot(block_i, rows_j, 1, 1)
            inter_t = dot(rows_j[chunk], rows_i, 1, 1)
            combined = ((2.0 * inter - inter_t) / (energy[t] - vir_sum)).astype(BF16)
            total = total + dot(combined, rows_j, 1, 0)
        for n in range(per):
            turn = jnp.transpose(total[n * lanes : (n + 1) * lanes])
            out[:, step * per + n] = turn.reshape(n_cyc, aux_blk, lanes).astype(BF16)
        part = pl.ds(step * per, per)
        stores.append(pltpu.make_async_copy(out.at[:, part], out_any.at[:, part], sems.at[4 + step]))
        stores[-1].start()
    for store in stores:
        store.wait()


def aux_kernel(place, dens, rows, near, far, acc):
    n_cyc, n_h, aux_blk, lanes = dens.shape
    sub, n_aux = rows.shape[2:]
    per = lanes // sub
    n_grp = near.shape[1]
    col_blk = n_aux // n_grp
    core = place[2]
    pad = jnp.zeros((lanes, lanes - col_blk), BF16)
    for h in range(n_h):
        block = rows[h * per : (h + 1) * per, 0].reshape(lanes, n_aux)
        pieces = []
        for g in range(n_grp):
            pieces += [block[:, g * col_blk : (g + 1) * col_blk], pad]
        left = dens[:, h].reshape(n_cyc * aux_blk, lanes)
        term = dot(left, jnp.concatenate(pieces, axis=1), 1, 0)
        if h == 0:
            acc[...] = term
        else:
            acc[...] += term

    def body(xy, carry):
        base = lax.div(xy, N_Y) * (2 * N_Y) + lax.rem(xy, N_Y)
        row = pl.multiple_of((base + N_Y * core) * aux_blk, 8)
        row_far = pl.multiple_of((base + N_Y * (1 - core)) * aux_blk, 8)
        for g in range(n_grp):
            cols = slice(g * lanes, (g + 1) * lanes)
            near[xy, g] = acc[pl.ds(row, aux_blk), cols]
            far[xy, g] = acc[pl.ds(row_far, aux_blk), cols].astype(BF16)
        return carry

    lax.fori_loop(0, n_cyc // 2, body, 0)


def fold_kernel(place, near, far, keep, send):
    n_half = keep.shape[1]
    yl = place[1]
    for g in range(n_half):
        mine = yl * n_half + g
        other = (1 - yl) * n_half + g
        keep[:, g] = near[:, mine] + far[:, mine].astype(F32)
        send[:, g] = (near[:, other] + far[:, other].astype(F32)).astype(BF16)


def lag_kernel(place, moved_any, ints, other_any, parts, wide, acc, moved, other_ints, sems):
    n_src, aux_blk, lanes = moved_any.shape
    n_orb = ints.shape[2]
    n_zl = parts.shape[2]
    n_cyc = n_src // n_zl
    shift, core = place[0], place[2]
    first = pltpu.make_async_copy(moved_any, moved, sems.at[0])
    first.start()
    loads = []
    per = aux_blk // N_LOAD
    for n in range(N_LOAD):
        part = pl.ds(n * per, per)
        loads.append(pltpu.make_async_copy(other_any.at[part], other_ints.at[part], sems.at[n + 1]))
        loads[n].start()
    first.wait()
    wide[...] = moved[...].reshape(n_src * aux_blk, lanes).astype(F32)
    for p in range(0, aux_blk, 2):
        if p % per == 0:
            loads[p // per].wait()
        left, right = [], []
        for q in (p, p + 1):
            x = wide[pl.ds(q, n_src, stride=aux_blk), :]
            left.append(pltpu.roll(x, core * (lanes // 2), 1).astype(BF16))
            right += [ints[q], other_ints[q]]
        term = dot(jnp.concatenate(left, axis=1), jnp.concatenate(right, axis=0), 1, 0)
        if p == 0:
            acc[...] = term
        else:
            acc[...] += term
    for k in range(n_cyc):
        target = lax.rem(k + shift, n_cyc)
        zh = lax.rem(lax.div(target, N_Y), 2)
        xy = lax.div(target, 2 * N_Y) * N_Y + lax.rem(target, N_Y)
        for g in range(n_orb // lanes):
            parts[xy * 2 + g % 2, zh, g // 2] = acc[k * n_zl : (k + 1) * n_zl, g * lanes : (g + 1) * lanes]


def join_kernel(lag, keep, recv, out):
    n_dest, n_zh, n_zl = lag.shape[:3]
    pieces = [lag[:, a, b] for a in range(n_zh) for b in range(n_zl)]
    n_lag = n_zh * n_zl * lag.shape[3]
    aux_blk, lanes = keep.shape[2:]
    n_low = keep.shape[1] // 2
    out[:, :n_lag] = jnp.concatenate(pieces, axis=1).astype(BF16)
    for xy in range(n_dest // 2):
        for low in range(n_low):
            for c in range(2):
                g = 2 * low + c
                out[2 * xy + c, n_lag + low * aux_blk : n_lag + (low + 1) * aux_blk] = (
                    keep[xy, g] + recv[xy, g].astype(F32)
                ).astype(BF16)


def plane_kernel(got, out):
    n_src = got.shape[0]
    n_z, n_rows, lanes = out.shape
    n_zl = n_z // 2
    n_lag = n_z * n_zl
    aux_blk = n_rows - 2 * n_zl
    n_low = (got.shape[1] - n_lag) // aux_blk
    for c in range(2):
        total = got[c, :n_lag].astype(F32)
        for src in range(c + 2, n_src, 2):
            total = total + got[src, :n_lag].astype(F32)
        for z in range(n_z):
            out[z, c * n_zl : (c + 1) * n_zl] = total[z * n_zl : (z + 1) * n_zl]
        for yl in range(2):
            first = 2 * yl + c
            total = got[first, n_lag:].astype(F32)
            for src in range(first + 4, n_src, 4):
                total = total + got[src, n_lag:].astype(F32)
            for low in range(n_low):
                z = c * n_zl + n_low * yl + low
                out[z, 2 * n_zl :] = total[low * aux_blk : (low + 1) * aux_blk]


def last_kernel(got, aux, lag):
    total = jnp.sum(got[...], axis=0)
    n_zl = lag.shape[0] // 2
    aux[...] = total[2 * n_zl :, : aux.shape[1]]
    for z in range(n_zl):
        for c in range(2):
            lag[2 * z + c : 2 * z + c + 1] = total[c * n_zl + z : c * n_zl + z + 1]


def local(b_factors, occ_energy, vir_energy, integrals, window_start):
    n_cyc = lax.axis_size(CYC)
    n_zl = lax.axis_size("zl")
    n_grp = n_zl * 2
    yl = lax.axis_index("yl")
    core = lax.axis_index("core")
    cyc = lax.axis_index(CYC)
    grp = lax.axis_index("zl") * 2 + core
    own = b_factors[0]
    n_vir, n_aux = own.shape
    n_orb = integrals.shape[2]
    aux_blk = n_aux // n_cyc
    shift = jnp.mod(window_start[0] + 1, n_cyc)
    place = jnp.stack([shift, yl, core]).astype(jnp.int32)

    mate = swap_yl(own)

    ints = jnp.transpose(integrals, (1, 0, 2))
    other_ints = swap_cores(ints)

    sub = n_vir // n_cyc
    spread = exchange_all(own.reshape(n_cyc, sub, n_aux), CYC)
    turned = call(
        turn_kernel,
        jax.ShapeDtypeStruct((n_cyc // 2, 2, 2, sub, n_aux), BF16),
        [pltpu.SemaphoreType.DMA((n_cyc + 4,))],
        0,
        8 * n_vir * n_aux,
        place,
        spread.reshape(n_cyc // 2, 2, sub, n_aux),
        specs=[smem, vmem],
        out_spec=hbm,
    )
    rows = exchange_all(turned.reshape(n_cyc, 2, sub, n_aux), CYC)

    step = 1 - 2 * yl
    energy_i = occ_energy[jnp.mod(cyc + shift, n_cyc) * n_grp + grp]
    energy_j = occ_energy[jnp.mod(cyc + jnp.stack([0, step, -step]), n_cyc) * n_grp + grp]
    dens = call(
        pair_kernel,
        jax.ShapeDtypeStruct((n_cyc, n_vir // LANES, aux_blk, LANES), BF16),
        [
            pltpu.VMEM((n_cyc, sub, n_aux), BF16),
            pltpu.VMEM((n_cyc, sub, n_aux), BF16),
            pltpu.VMEM((n_vir, n_aux), BF16),
            pltpu.VMEM((n_vir, n_aux), BF16),
            pltpu.VMEM((n_cyc, n_vir // LANES, aux_blk, LANES), BF16),
            pltpu.SemaphoreType.DMA((4 + N_STEP,)),
        ],
        18 * n_vir * n_vir * n_aux,
        5 * 2 * n_vir * n_aux,
        energy_i + energy_j,
        vir_energy[None, :],
        vir_energy[:, None],
        rows,
        own,
        mate,
        specs=[smem, vmem, vmem, hbm, hbm, hbm],
        out_spec=hbm,
        grant=PAIR_BYTES,
    )
    moved = exchange_all(dens.reshape(n_cyc * n_zl, aux_blk, LANES), CYC + ("zl",))

    n_xy = n_cyc // 2
    near, far = call(
        aux_kernel,
        (
            jax.ShapeDtypeStruct((n_xy, n_grp, aux_blk, LANES), F32),
            jax.ShapeDtypeStruct((n_xy, n_grp, aux_blk, LANES), BF16),
        ),
        [pltpu.VMEM((n_aux, n_grp * LANES), F32)],
        2 * n_vir * n_aux * n_aux,
        10 * n_vir * n_aux,
        place,
        dens,
        rows,
        specs=[smem, vmem, vmem],
    )
    keep, send = call(
        fold_kernel,
        (
            jax.ShapeDtypeStruct((n_xy, n_grp // 2, aux_blk, LANES), F32),
            jax.ShapeDtypeStruct((n_xy, n_grp // 2, aux_blk, LANES), BF16),
        ),
        [],
        0,
        9 * n_vir * n_aux,
        place,
        near,
        swap_cores(far),
        specs=[smem, vmem, vmem],
    )
    recv = swap_yl(send)

    lag = call(
        lag_kernel,
        jax.ShapeDtypeStruct((n_cyc, 2, n_zl, n_zl, LANES), F32),
        [
            pltpu.VMEM((n_vir * n_aux // LANES, LANES), F32),
            pltpu.VMEM((n_cyc * n_zl, n_orb), F32),
            pltpu.VMEM((n_cyc * n_zl, aux_blk, LANES), BF16),
            pltpu.VMEM(ints.shape, BF16),
            pltpu.SemaphoreType.DMA((1 + N_LOAD,)),
        ],
        2 * n_vir * n_aux * n_orb,
        2 * n_vir * n_aux * 10,
        place,
        moved,
        ints,
        other_ints,
        specs=[smem, hbm, vmem, hbm],
    )
    n_rows = 2 * n_zl * n_zl + n_zl // 2 * aux_blk
    parts = call(
        join_kernel,
        jax.ShapeDtypeStruct((n_cyc, n_rows, LANES), BF16),
        [],
        0,
        8 * n_cyc * n_rows * LANES,
        lag,
        keep,
        recv,
        specs=[vmem] * 3,
    )
    plane = call(
        plane_kernel,
        jax.ShapeDtypeStruct((2 * n_zl, n_grp + aux_blk, LANES), F32),
        [],
        n_cyc * n_rows * LANES,
        2 * n_cyc * n_rows * LANES,
        exchange_all(parts, PLANE),
        specs=[vmem],
    )
    aux_metric, lagrangian = call(
        last_kernel,
        (jax.ShapeDtypeStruct((aux_blk, n_aux // n_grp), F32), jax.ShapeDtypeStruct((n_grp, LANES), F32)),
        [],
        0,
        4 * 2 * n_zl * 32 * LANES,
        exchange_all(plane, DEPTH),
        specs=[vmem],
    )
    return (aux_metric, lagrangian)


def solution(mesh):
    n_occ, n_grp = mesh.shape["occ"], mesh.shape["grp"]
    sizes = (n_occ // (2 * N_Y), 2, N_Y // 2, 2, n_grp // 2, 2)
    fine = Mesh(mesh.devices.reshape(sizes), CYC + ("zl", "core"))
    grp = ("zl", "core")
    placed = (P(CYC + grp, None, None), P(), P(), P(grp, CYC, None), P())
    return jax.shard_map(
        local,
        mesh=fine,
        in_specs=placed,
        out_specs=(P(CYC, grp), P(CYC, grp)),
        check_vma=False,
    )
```

```python
import jax
import jax.numpy as jnp
from jax import lax
from jax.experimental import pallas as pl
from jax.experimental.pallas import tpu as pltpu
from jax.sharding import Mesh, PartitionSpec as P

BF16 = jnp.bfloat16
F32 = jnp.float32
LANES = 128
VMEM_BYTES = 40 * 1024 * 1024
CYC = ("x", "zh", "yh", "yl")
PLANE = ("x", "yh", "yl", "core")
DEPTH = ("zh", "zl")
N_Y = 4
N_LOAD = 4

vmem = pl.BlockSpec(memory_space=pltpu.VMEM)
smem = pl.BlockSpec(memory_space=pltpu.SMEM)
hbm = pl.BlockSpec(memory_space=pl.ANY)


def exchange_all(x, axes):
    return lax.all_to_all(x, axes, split_axis=0, concat_axis=0, tiled=True)


def swap_cores(x):
    return lax.ppermute(x, "core", [(0, 1), (1, 0)])


def swap_yl(x):
    return lax.ppermute(x, "yl", [(0, 1), (1, 0)])


def dot(a, b, ca, cb):
    return lax.dot_general(a, b, (((ca,), (cb,)), ((), ())), preferred_element_type=F32)


def call(kernel, outs, scratch, flops, nbytes, *args, specs):
    return pl.pallas_call(
        kernel,
        out_shape=outs,
        in_specs=specs,
        out_specs=jax.tree.map(lambda _: vmem, outs),
        scratch_shapes=scratch,
        compiler_params=pltpu.CompilerParams(vmem_limit_bytes=VMEM_BYTES),
        cost_estimate=pl.CostEstimate(flops=flops, bytes_accessed=nbytes, transcendentals=0),
    )(*args)


def turn_kernel(place, spread, out):
    n_cyc = spread.shape[0]
    shift = place[0]

    def body(pair, carry):
        for odd in range(2):
            d = 2 * pair + odd
            out[d, 0] = spread[lax.rem(d + shift, n_cyc)]
            out[d, 1] = spread[lax.rem(d + (2 * odd - 1) + n_cyc, n_cyc)]
        return carry

    lax.fori_loop(0, n_cyc // 2, body, 0)


def pair_kernel(energy, vir_row, vir_col, rows, own, mate, out):
    n_cyc, n_h, aux_blk, lanes = out.shape
    n_vir, n_aux = own.shape
    rows_i = rows[:, 0].reshape(n_vir, n_aux)
    vir_sum = vir_col[...] + vir_row[...]
    total = jnp.zeros((n_vir, n_aux), F32)
    for t, rows_j in enumerate((own[...], mate[...], rows[:, 1].reshape(n_vir, n_aux))):
        inter = dot(rows_i, rows_j, 1, 1)
        combined = ((2.0 * inter - jnp.transpose(inter)) / (energy[t] - vir_sum)).astype(BF16)
        total = total + dot(combined, rows_j, 1, 0)
    for h in range(n_h):
        turned = jnp.transpose(total[h * lanes : (h + 1) * lanes])
        out[:, h] = turned.reshape(n_cyc, aux_blk, lanes).astype(BF16)


def aux_kernel(place, dens, rows, near, far, acc):
    n_cyc, n_h, aux_blk, lanes = dens.shape
    sub, n_aux = rows.shape[2:]
    per = lanes // sub
    n_grp = near.shape[1]
    col_blk = n_aux // n_grp
    core = place[2]
    pad = jnp.zeros((lanes, lanes - col_blk), BF16)
    for h in range(n_h):
        block = rows[h * per : (h + 1) * per, 0].reshape(lanes, n_aux)
        pieces = []
        for g in range(n_grp):
            pieces += [block[:, g * col_blk : (g + 1) * col_blk], pad]
        left = dens[:, h].reshape(n_cyc * aux_blk, lanes)
        term = dot(left, jnp.concatenate(pieces, axis=1), 1, 0)
        if h == 0:
            acc[...] = term
        else:
            acc[...] += term

    def body(xy, carry):
        base = lax.div(xy, N_Y) * (2 * N_Y) + lax.rem(xy, N_Y)
        row = pl.multiple_of((base + N_Y * core) * aux_blk, 8)
        row_far = pl.multiple_of((base + N_Y * (1 - core)) * aux_blk, 8)
        for g in range(n_grp):
            cols = slice(g * lanes, (g + 1) * lanes)
            near[xy, g] = acc[pl.ds(row, aux_blk), cols]
            far[xy, g] = acc[pl.ds(row_far, aux_blk), cols].astype(BF16)
        return carry

    lax.fori_loop(0, n_cyc // 2, body, 0)


def fold_kernel(place, near, far, keep, send):
    n_half = keep.shape[1]
    yl = place[1]
    for g in range(n_half):
        mine = yl * n_half + g
        other = (1 - yl) * n_half + g
        keep[:, g] = near[:, mine] + far[:, mine].astype(F32)
        send[:, g] = (near[:, other] + far[:, other].astype(F32)).astype(BF16)


def lag_kernel(place, moved_any, ints, other_any, parts, wide, acc, moved, other_ints, sems):
    n_src, aux_blk, lanes = moved_any.shape
    n_orb = ints.shape[2]
    n_zl = parts.shape[2]
    n_cyc = n_src // n_zl
    shift, core = place[0], place[2]
    first = pltpu.make_async_copy(moved_any, moved, sems.at[0])
    first.start()
    loads = []
    per = aux_blk // N_LOAD
    for n in range(N_LOAD):
        part = pl.ds(n * per, per)
        loads.append(pltpu.make_async_copy(other_any.at[part], other_ints.at[part], sems.at[n + 1]))
        loads[n].start()
    first.wait()
    wide[...] = moved[...].reshape(n_src * aux_blk, lanes).astype(F32)
    for p in range(0, aux_blk, 2):
        if p % per == 0:
            loads[p // per].wait()
        left, right = [], []
        for q in (p, p + 1):
            x = wide[pl.ds(q, n_src, stride=aux_blk), :]
            left.append(pltpu.roll(x, core * (lanes // 2), 1).astype(BF16))
            right += [ints[q], other_ints[q]]
        term = dot(jnp.concatenate(left, axis=1), jnp.concatenate(right, axis=0), 1, 0)
        if p == 0:
            acc[...] = term
        else:
            acc[...] += term
    for k in range(n_cyc):
        target = lax.rem(k + shift, n_cyc)
        zh = lax.rem(lax.div(target, N_Y), 2)
        xy = lax.div(target, 2 * N_Y) * N_Y + lax.rem(target, N_Y)
        for g in range(n_orb // lanes):
            parts[xy * 2 + g % 2, zh, g // 2] = acc[k * n_zl : (k + 1) * n_zl, g * lanes : (g + 1) * lanes]


def join_kernel(lag, keep, recv, out):
    n_dest, n_zh, n_zl = lag.shape[:3]
    pieces = [lag[:, a, b] for a in range(n_zh) for b in range(n_zl)]
    n_lag = n_zh * n_zl * lag.shape[3]
    aux_blk, lanes = keep.shape[2:]
    n_low = keep.shape[1] // 2
    out[:, :n_lag] = jnp.concatenate(pieces, axis=1).astype(BF16)
    for xy in range(n_dest // 2):
        for low in range(n_low):
            for c in range(2):
                g = 2 * low + c
                out[2 * xy + c, n_lag + low * aux_blk : n_lag + (low + 1) * aux_blk] = (
                    keep[xy, g] + recv[xy, g].astype(F32)
                ).astype(BF16)


def plane_kernel(got, out):
    n_src = got.shape[0]
    n_z, n_rows, lanes = out.shape
    n_zl = n_z // 2
    n_lag = n_z * n_zl
    aux_blk = n_rows - 2 * n_zl
    n_low = (got.shape[1] - n_lag) // aux_blk
    for c in range(2):
        total = got[c, :n_lag].astype(F32)
        for src in range(c + 2, n_src, 2):
            total = total + got[src, :n_lag].astype(F32)
        for z in range(n_z):
            out[z, c * n_zl : (c + 1) * n_zl] = total[z * n_zl : (z + 1) * n_zl]
        for yl in range(2):
            first = 2 * yl + c
            total = got[first, n_lag:].astype(F32)
            for src in range(first + 4, n_src, 4):
                total = total + got[src, n_lag:].astype(F32)
            for low in range(n_low):
                z = c * n_zl + n_low * yl + low
                out[z, 2 * n_zl :] = total[low * aux_blk : (low + 1) * aux_blk]


def last_kernel(got, aux, lag):
    total = jnp.sum(got[...], axis=0)
    n_zl = lag.shape[0] // 2
    aux[...] = total[2 * n_zl :, : aux.shape[1]]
    for z in range(n_zl):
        for c in range(2):
            lag[2 * z + c : 2 * z + c + 1] = total[c * n_zl + z : c * n_zl + z + 1]


def local(b_factors, occ_energy, vir_energy, integrals, window_start):
    n_cyc = lax.axis_size(CYC)
    n_zl = lax.axis_size("zl")
    n_grp = n_zl * 2
    yl = lax.axis_index("yl")
    core = lax.axis_index("core")
    cyc = lax.axis_index(CYC)
    grp = lax.axis_index("zl") * 2 + core
    own = b_factors[0]
    n_vir, n_aux = own.shape
    n_orb = integrals.shape[2]
    aux_blk = n_aux // n_cyc
    shift = jnp.mod(window_start[0] + 1, n_cyc)
    place = jnp.stack([shift, yl, core]).astype(jnp.int32)

    mate = swap_yl(own)

    ints = jnp.transpose(integrals, (1, 0, 2))
    other_ints = swap_cores(ints)

    sub = n_vir // n_cyc
    spread = exchange_all(own.reshape(n_cyc, sub, n_aux), CYC)
    turned = call(
        turn_kernel,
        jax.ShapeDtypeStruct((n_cyc, 2, sub, n_aux), BF16),
        [],
        0,
        8 * n_vir * n_aux,
        place,
        spread,
        specs=[smem, vmem],
    )
    rows = exchange_all(turned, CYC)

    step = 1 - 2 * yl
    energy_i = occ_energy[jnp.mod(cyc + shift, n_cyc) * n_grp + grp]
    energy_j = occ_energy[jnp.mod(cyc + jnp.stack([0, step, -step]), n_cyc) * n_grp + grp]
    dens = call(
        pair_kernel,
        jax.ShapeDtypeStruct((n_cyc, n_vir // LANES, aux_blk, LANES), BF16),
        [],
        18 * n_vir * n_vir * n_aux,
        5 * 2 * n_vir * n_aux,
        energy_i + energy_j,
        vir_energy[None, :],
        vir_energy[:, None],
        rows,
        own,
        mate,
        specs=[smem] + [vmem] * 5,
    )
    moved = exchange_all(dens.reshape(n_cyc * n_zl, aux_blk, LANES), CYC + ("zl",))

    n_xy = n_cyc // 2
    near, far = call(
        aux_kernel,
        (
            jax.ShapeDtypeStruct((n_xy, n_grp, aux_blk, LANES), F32),
            jax.ShapeDtypeStruct((n_xy, n_grp, aux_blk, LANES), BF16),
        ),
        [pltpu.VMEM((n_aux, n_grp * LANES), F32)],
        2 * n_vir * n_aux * n_aux,
        10 * n_vir * n_aux,
        place,
        dens,
        rows,
        specs=[smem, vmem, vmem],
    )
    keep, send = call(
        fold_kernel,
        (
            jax.ShapeDtypeStruct((n_xy, n_grp // 2, aux_blk, LANES), F32),
            jax.ShapeDtypeStruct((n_xy, n_grp // 2, aux_blk, LANES), BF16),
        ),
        [],
        0,
        9 * n_vir * n_aux,
        place,
        near,
        swap_cores(far),
        specs=[smem, vmem, vmem],
    )
    recv = swap_yl(send)

    lag = call(
        lag_kernel,
        jax.ShapeDtypeStruct((n_cyc, 2, n_zl, n_zl, LANES), F32),
        [
            pltpu.VMEM((n_vir * n_aux // LANES, LANES), F32),
            pltpu.VMEM((n_cyc * n_zl, n_orb), F32),
            pltpu.VMEM((n_cyc * n_zl, aux_blk, LANES), BF16),
            pltpu.VMEM(ints.shape, BF16),
            pltpu.SemaphoreType.DMA((1 + N_LOAD,)),
        ],
        2 * n_vir * n_aux * n_orb,
        2 * n_vir * n_aux * 10,
        place,
        moved,
        ints,
        other_ints,
        specs=[smem, hbm, vmem, hbm],
    )
    n_rows = 2 * n_zl * n_zl + n_zl // 2 * aux_blk
    parts = call(
        join_kernel,
        jax.ShapeDtypeStruct((n_cyc, n_rows, LANES), BF16),
        [],
        0,
        8 * n_cyc * n_rows * LANES,
        lag,
        keep,
        recv,
        specs=[vmem] * 3,
    )
    plane = call(
        plane_kernel,
        jax.ShapeDtypeStruct((2 * n_zl, n_grp + aux_blk, LANES), F32),
        [],
        n_cyc * n_rows * LANES,
        2 * n_cyc * n_rows * LANES,
        exchange_all(parts, PLANE),
        specs=[vmem],
    )
    aux_metric, lagrangian = call(
        last_kernel,
        (jax.ShapeDtypeStruct((aux_blk, n_aux // n_grp), F32), jax.ShapeDtypeStruct((n_grp, LANES), F32)),
        [],
        0,
        4 * 2 * n_zl * 32 * LANES,
        exchange_all(plane, DEPTH),
        specs=[vmem],
    )
    return (aux_metric, lagrangian)


def solution(mesh):
    n_occ, n_grp = mesh.shape["occ"], mesh.shape["grp"]
    sizes = (n_occ // (2 * N_Y), 2, N_Y // 2, 2, n_grp // 2, 2)
    fine = Mesh(mesh.devices.reshape(sizes), CYC + ("zl", "core"))
    grp = ("zl", "core")
    placed = (P(CYC + grp, None, None), P(), P(), P(grp, CYC, None), P())
    return jax.shard_map(
        local,
        mesh=fine,
        in_specs=placed,
        out_specs=(P(CYC, grp), P(CYC, grp)),
        check_vma=False,
    )
```

```python
import jax
import jax.numpy as jnp
from jax import lax
from jax.experimental import pallas as pl
from jax.experimental.pallas import tpu as pltpu
from jax.sharding import Mesh, PartitionSpec as P

BF16 = jnp.bfloat16
F32 = jnp.float32
LANES = 128
VMEM_BYTES = 50 * 1024 * 1024
CYC = ("x", "zh", "yh", "yl")
PLANE = ("x", "yh", "yl", "core")
DEPTH = ("zh", "zl")
N_Y = 4
N_LOAD = 4

vmem = pl.BlockSpec(memory_space=pltpu.VMEM)
smem = pl.BlockSpec(memory_space=pltpu.SMEM)
hbm = pl.BlockSpec(memory_space=pl.ANY)


def exchange_all(x, axes):
    return lax.all_to_all(x, axes, split_axis=0, concat_axis=0, tiled=True)


def swap_cores(x):
    return lax.ppermute(x, "core", [(0, 1), (1, 0)])


def swap_yl(x):
    return lax.ppermute(x, "yl", [(0, 1), (1, 0)])


def dot(a, b, ca, cb):
    return lax.dot_general(a, b, (((ca,), (cb,)), ((), ())), preferred_element_type=F32)


def call(kernel, outs, scratch, flops, nbytes, *args, specs):
    return pl.pallas_call(
        kernel,
        out_shape=outs,
        in_specs=specs,
        out_specs=jax.tree.map(lambda _: vmem, outs),
        scratch_shapes=scratch,
        compiler_params=pltpu.CompilerParams(vmem_limit_bytes=VMEM_BYTES),
        cost_estimate=pl.CostEstimate(flops=flops, bytes_accessed=nbytes, transcendentals=0),
    )(*args)


def turn_kernel(place, spread, out):
    n_cyc = spread.shape[0]
    shift = place[0]

    def body(pair, carry):
        for odd in range(2):
            d = 2 * pair + odd
            out[d, 0] = spread[lax.rem(d + shift, n_cyc)]
            out[d, 1] = spread[lax.rem(d + (2 * odd - 1) + n_cyc, n_cyc)]
        return carry

    lax.fori_loop(0, n_cyc // 2, body, 0)


def pair_kernel(energy, vir_row, vir_col, rows, own, mate, out):
    n_cyc, n_h, aux_blk, lanes = out.shape
    n_vir, n_aux = own.shape
    rows_i = rows[:, 0].reshape(n_vir, n_aux)
    vir_sum = vir_col[...] + vir_row[...]
    total = jnp.zeros((n_vir, n_aux), F32)
    for t, rows_j in enumerate((own[...], mate[...], rows[:, 1].reshape(n_vir, n_aux))):
        inter = dot(rows_i, rows_j, 1, 1)
        combined = ((2.0 * inter - jnp.transpose(inter)) / (energy[t] - vir_sum)).astype(BF16)
        total = total + dot(combined, rows_j, 1, 0)
    for h in range(n_h):
        turned = jnp.transpose(total[h * lanes : (h + 1) * lanes])
        out[:, h] = turned.reshape(n_cyc, aux_blk, lanes).astype(BF16)


def aux_kernel(place, dens, rows, near, far, acc):
    n_cyc, n_h, aux_blk, lanes = dens.shape
    sub, n_aux = rows.shape[2:]
    per = lanes // sub
    n_grp = near.shape[1]
    col_blk = n_aux // n_grp
    core = place[2]
    pad = jnp.zeros((lanes, lanes - col_blk), BF16)
    for h in range(n_h):
        block = rows[h * per : (h + 1) * per, 0].reshape(lanes, n_aux)
        pieces = []
        for g in range(n_grp):
            pieces += [block[:, g * col_blk : (g + 1) * col_blk], pad]
        left = dens[:, h].reshape(n_cyc * aux_blk, lanes)
        term = dot(left, jnp.concatenate(pieces, axis=1), 1, 0)
        if h == 0:
            acc[...] = term
        else:
            acc[...] += term

    def body(xy, carry):
        base = lax.div(xy, N_Y) * (2 * N_Y) + lax.rem(xy, N_Y)
        row = pl.multiple_of((base + N_Y * core) * aux_blk, 8)
        row_far = pl.multiple_of((base + N_Y * (1 - core)) * aux_blk, 8)
        for g in range(n_grp):
            cols = slice(g * lanes, (g + 1) * lanes)
            near[xy, g] = acc[pl.ds(row, aux_blk), cols]
            far[xy, g] = acc[pl.ds(row_far, aux_blk), cols].astype(BF16)
        return carry

    lax.fori_loop(0, n_cyc // 2, body, 0)


def fold_kernel(place, near, far, keep, send):
    n_half = keep.shape[1]
    yl = place[1]
    for g in range(n_half):
        mine = yl * n_half + g
        other = (1 - yl) * n_half + g
        keep[:, g] = near[:, mine] + far[:, mine].astype(F32)
        send[:, g] = (near[:, other] + far[:, other].astype(F32)).astype(BF16)


def lag_kernel(place, moved_any, ints_any, other_any, parts, wide, acc, moved, ints, other_ints, sems):
    n_src, aux_blk, lanes = moved_any.shape
    n_orb = ints_any.shape[2]
    n_zl = parts.shape[2]
    n_cyc = n_src // n_zl
    shift, core = place[0], place[2]
    first = pltpu.make_async_copy(moved_any, moved, sems.at[0])
    first.start()
    loads = []
    per = aux_blk // N_LOAD
    for n in range(N_LOAD):
        part = pl.ds(n * per, per)
        for src, dst in ((ints_any, ints), (other_any, other_ints)):
            loads.append(pltpu.make_async_copy(src.at[part], dst.at[part], sems.at[len(loads) + 1]))
            loads[-1].start()
    first.wait()
    wide[...] = moved[...].reshape(n_src * aux_blk, lanes).astype(F32)
    for p in range(0, aux_blk, 2):
        if p % per == 0:
            loads[p // per * 2].wait()
            loads[p // per * 2 + 1].wait()
        left, right = [], []
        for q in (p, p + 1):
            x = wide[pl.ds(q, n_src, stride=aux_blk), :]
            left.append(pltpu.roll(x, core * (lanes // 2), 1).astype(BF16))
            right += [ints[q], other_ints[q]]
        term = dot(jnp.concatenate(left, axis=1), jnp.concatenate(right, axis=0), 1, 0)
        if p == 0:
            acc[...] = term
        else:
            acc[...] += term
    for k in range(n_cyc):
        target = lax.rem(k + shift, n_cyc)
        zh = lax.rem(lax.div(target, N_Y), 2)
        xy = lax.div(target, 2 * N_Y) * N_Y + lax.rem(target, N_Y)
        for g in range(n_orb // lanes):
            parts[xy * 2 + g % 2, zh, g // 2] = acc[k * n_zl : (k + 1) * n_zl, g * lanes : (g + 1) * lanes]


def join_kernel(lag, keep, recv, out):
    n_dest, n_zh, n_zl = lag.shape[:3]
    pieces = [lag[:, a, b] for a in range(n_zh) for b in range(n_zl)]
    n_lag = n_zh * n_zl * lag.shape[3]
    aux_blk, lanes = keep.shape[2:]
    n_low = keep.shape[1] // 2
    out[:, :n_lag] = jnp.concatenate(pieces, axis=1).astype(BF16)
    for xy in range(n_dest // 2):
        for low in range(n_low):
            for c in range(2):
                g = 2 * low + c
                out[2 * xy + c, n_lag + low * aux_blk : n_lag + (low + 1) * aux_blk] = (
                    keep[xy, g] + recv[xy, g].astype(F32)
                ).astype(BF16)


def plane_kernel(got, out):
    n_src = got.shape[0]
    n_z, n_rows, lanes = out.shape
    n_zl = n_z // 2
    n_lag = n_z * n_zl
    aux_blk = n_rows - 2 * n_zl
    n_low = (got.shape[1] - n_lag) // aux_blk
    for c in range(2):
        total = got[c, :n_lag].astype(F32)
        for src in range(c + 2, n_src, 2):
            total = total + got[src, :n_lag].astype(F32)
        for z in range(n_z):
            out[z, c * n_zl : (c + 1) * n_zl] = total[z * n_zl : (z + 1) * n_zl]
        for yl in range(2):
            first = 2 * yl + c
            total = got[first, n_lag:].astype(F32)
            for src in range(first + 4, n_src, 4):
                total = total + got[src, n_lag:].astype(F32)
            for low in range(n_low):
                z = c * n_zl + n_low * yl + low
                out[z, 2 * n_zl :] = total[low * aux_blk : (low + 1) * aux_blk]


def last_kernel(got, aux, lag):
    total = jnp.sum(got[...], axis=0)
    n_zl = lag.shape[0] // 2
    aux[...] = total[2 * n_zl :, : aux.shape[1]]
    for z in range(n_zl):
        for c in range(2):
            lag[2 * z + c : 2 * z + c + 1] = total[c * n_zl + z : c * n_zl + z + 1]


def local(b_factors, occ_energy, vir_energy, integrals, window_start):
    n_cyc = lax.axis_size(CYC)
    n_zl = lax.axis_size("zl")
    n_grp = n_zl * 2
    yl = lax.axis_index("yl")
    core = lax.axis_index("core")
    cyc = lax.axis_index(CYC)
    grp = lax.axis_index("zl") * 2 + core
    own = b_factors[0]
    n_vir, n_aux = own.shape
    n_orb = integrals.shape[2]
    aux_blk = n_aux // n_cyc
    shift = jnp.mod(window_start[0] + 1, n_cyc)
    place = jnp.stack([shift, yl, core]).astype(jnp.int32)

    mate = swap_yl(own)

    ints = jnp.transpose(integrals, (1, 0, 2))
    ints, other_ints, mate = lax.optimization_barrier((ints, swap_cores(ints), mate))

    sub = n_vir // n_cyc
    spread = exchange_all(own.reshape(n_cyc, sub, n_aux), CYC)
    turned = call(
        turn_kernel,
        jax.ShapeDtypeStruct((n_cyc, 2, sub, n_aux), BF16),
        [],
        0,
        8 * n_vir * n_aux,
        place,
        spread,
        specs=[smem, vmem],
    )
    rows = exchange_all(turned, CYC)

    step = 1 - 2 * yl
    energy_i = occ_energy[jnp.mod(cyc + shift, n_cyc) * n_grp + grp]
    energy_j = occ_energy[jnp.mod(cyc + jnp.stack([0, step, -step]), n_cyc) * n_grp + grp]
    dens = call(
        pair_kernel,
        jax.ShapeDtypeStruct((n_cyc, n_vir // LANES, aux_blk, LANES), BF16),
        [],
        18 * n_vir * n_vir * n_aux,
        5 * 2 * n_vir * n_aux,
        energy_i + energy_j,
        vir_energy[None, :],
        vir_energy[:, None],
        rows,
        own,
        mate,
        specs=[smem] + [vmem] * 5,
    )
    moved = exchange_all(dens.reshape(n_cyc * n_zl, aux_blk, LANES), CYC + ("zl",))

    n_xy = n_cyc // 2
    near, far = call(
        aux_kernel,
        (
            jax.ShapeDtypeStruct((n_xy, n_grp, aux_blk, LANES), F32),
            jax.ShapeDtypeStruct((n_xy, n_grp, aux_blk, LANES), BF16),
        ),
        [pltpu.VMEM((n_aux, n_grp * LANES), F32)],
        2 * n_vir * n_aux * n_aux,
        10 * n_vir * n_aux,
        place,
        dens,
        rows,
        specs=[smem, vmem, vmem],
    )
    keep, send = call(
        fold_kernel,
        (
            jax.ShapeDtypeStruct((n_xy, n_grp // 2, aux_blk, LANES), F32),
            jax.ShapeDtypeStruct((n_xy, n_grp // 2, aux_blk, LANES), BF16),
        ),
        [],
        0,
        9 * n_vir * n_aux,
        place,
        near,
        swap_cores(far),
        specs=[smem, vmem, vmem],
    )
    recv = swap_yl(send)

    lag = call(
        lag_kernel,
        jax.ShapeDtypeStruct((n_cyc, 2, n_zl, n_zl, LANES), F32),
        [
            pltpu.VMEM((n_vir * n_aux // LANES, LANES), F32),
            pltpu.VMEM((n_cyc * n_zl, n_orb), F32),
            pltpu.VMEM((n_cyc * n_zl, aux_blk, LANES), BF16),
            pltpu.VMEM(ints.shape, BF16),
            pltpu.VMEM(ints.shape, BF16),
            pltpu.SemaphoreType.DMA((1 + 2 * N_LOAD,)),
        ],
        2 * n_vir * n_aux * n_orb,
        2 * n_vir * n_aux * 10,
        place,
        moved,
        ints,
        other_ints,
        specs=[smem, hbm, hbm, hbm],
    )
    n_rows = 2 * n_zl * n_zl + n_zl // 2 * aux_blk
    parts = call(
        join_kernel,
        jax.ShapeDtypeStruct((n_cyc, n_rows, LANES), BF16),
        [],
        0,
        8 * n_cyc * n_rows * LANES,
        lag,
        keep,
        recv,
        specs=[vmem] * 3,
    )
    plane = call(
        plane_kernel,
        jax.ShapeDtypeStruct((2 * n_zl, n_grp + aux_blk, LANES), F32),
        [],
        n_cyc * n_rows * LANES,
        2 * n_cyc * n_rows * LANES,
        exchange_all(parts, PLANE),
        specs=[vmem],
    )
    aux_metric, lagrangian = call(
        last_kernel,
        (jax.ShapeDtypeStruct((aux_blk, n_aux // n_grp), F32), jax.ShapeDtypeStruct((n_grp, LANES), F32)),
        [],
        0,
        4 * 2 * n_zl * 32 * LANES,
        exchange_all(plane, DEPTH),
        specs=[vmem],
    )
    return (aux_metric, lagrangian)


def solution(mesh):
    n_occ, n_grp = mesh.shape["occ"], mesh.shape["grp"]
    sizes = (n_occ // (2 * N_Y), 2, N_Y // 2, 2, n_grp // 2, 2)
    fine = Mesh(mesh.devices.reshape(sizes), CYC + ("zl", "core"))
    grp = ("zl", "core")
    placed = (P(CYC + grp, None, None), P(), P(), P(grp, CYC, None), P())
    return jax.shard_map(
        local,
        mesh=fine,
        in_specs=placed,
        out_specs=(P(CYC, grp), P(CYC, grp)),
        check_vma=False,
    )
```

```python
import jax
import jax.numpy as jnp
from jax import lax
from jax.experimental import pallas as pl
from jax.experimental.pallas import tpu as pltpu
from jax.sharding import Mesh, PartitionSpec as P

BF16 = jnp.bfloat16
F32 = jnp.float32
LANES = 128
VMEM_BYTES = 50 * 1024 * 1024
CYC = ("x", "zh", "yh", "yl")
PLANE = ("x", "yh", "yl", "core")
DEPTH = ("zh", "zl")
N_Y = 4
N_LOAD = 6

vmem = pl.BlockSpec(memory_space=pltpu.VMEM)
smem = pl.BlockSpec(memory_space=pltpu.SMEM)
hbm = pl.BlockSpec(memory_space=pl.ANY)


def exchange_all(x, axes):
    return lax.all_to_all(x, axes, split_axis=0, concat_axis=0, tiled=True)


def swap_cores(x):
    return lax.ppermute(x, "core", [(0, 1), (1, 0)])


def swap_yl(x):
    return lax.ppermute(x, "yl", [(0, 1), (1, 0)])


def dot(a, b, ca, cb):
    return lax.dot_general(a, b, (((ca,), (cb,)), ((), ())), preferred_element_type=F32)


def call(kernel, outs, scratch, flops, nbytes, *args, specs):
    return pl.pallas_call(
        kernel,
        out_shape=outs,
        in_specs=specs,
        out_specs=jax.tree.map(lambda _: vmem, outs),
        scratch_shapes=scratch,
        compiler_params=pltpu.CompilerParams(vmem_limit_bytes=VMEM_BYTES),
        cost_estimate=pl.CostEstimate(flops=flops, bytes_accessed=nbytes, transcendentals=0),
    )(*args)


def turn_kernel(place, spread, out):
    n_cyc = spread.shape[0]
    shift = place[0]

    def body(pair, carry):
        for odd in range(2):
            d = 2 * pair + odd
            out[d, 0] = spread[lax.rem(d + shift, n_cyc)]
            out[d, 1] = spread[lax.rem(d + (2 * odd - 1) + n_cyc, n_cyc)]
        return carry

    lax.fori_loop(0, n_cyc // 2, body, 0)


def pair_kernel(energy, vir_row, vir_col, rows, own, mate, out):
    n_cyc, n_h, aux_blk, lanes = out.shape
    n_vir, n_aux = own.shape
    rows_i = rows[:, 0].reshape(n_vir, n_aux)
    vir_sum = vir_col[...] + vir_row[...]
    total = jnp.zeros((n_vir, n_aux), F32)
    for t, rows_j in enumerate((own[...], mate[...], rows[:, 1].reshape(n_vir, n_aux))):
        inter = dot(rows_i, rows_j, 1, 1)
        combined = ((2.0 * inter - jnp.transpose(inter)) / (energy[t] - vir_sum)).astype(BF16)
        total = total + dot(combined, rows_j, 1, 0)
    for h in range(n_h):
        turned = jnp.transpose(total[h * lanes : (h + 1) * lanes])
        out[:, h] = turned.reshape(n_cyc, aux_blk, lanes).astype(BF16)


def aux_kernel(place, dens, rows, near, far, acc):
    n_cyc, n_h, aux_blk, lanes = dens.shape
    sub, n_aux = rows.shape[2:]
    per = lanes // sub
    n_grp = near.shape[1]
    col_blk = n_aux // n_grp
    core = place[2]
    pad = jnp.zeros((lanes, lanes - col_blk), BF16)
    for h in range(n_h):
        block = rows[h * per : (h + 1) * per, 0].reshape(lanes, n_aux)
        pieces = []
        for g in range(n_grp):
            pieces += [block[:, g * col_blk : (g + 1) * col_blk], pad]
        left = dens[:, h].reshape(n_cyc * aux_blk, lanes)
        term = dot(left, jnp.concatenate(pieces, axis=1), 1, 0)
        if h == 0:
            acc[...] = term
        else:
            acc[...] += term

    def body(xy, carry):
        base = lax.div(xy, N_Y) * (2 * N_Y) + lax.rem(xy, N_Y)
        row = pl.multiple_of((base + N_Y * core) * aux_blk, 8)
        row_far = pl.multiple_of((base + N_Y * (1 - core)) * aux_blk, 8)
        for g in range(n_grp):
            cols = slice(g * lanes, (g + 1) * lanes)
            near[xy, g] = acc[pl.ds(row, aux_blk), cols]
            far[xy, g] = acc[pl.ds(row_far, aux_blk), cols].astype(BF16)
        return carry

    lax.fori_loop(0, n_cyc // 2, body, 0)


def fold_kernel(place, near, far, keep, send):
    n_half = keep.shape[1]
    yl = place[1]
    for g in range(n_half):
        mine = yl * n_half + g
        other = (1 - yl) * n_half + g
        keep[:, g] = near[:, mine] + far[:, mine].astype(F32)
        send[:, g] = (near[:, other] + far[:, other].astype(F32)).astype(BF16)


def lag_kernel(place, moved, ints_any, other_any, parts, wide, acc, ints, other_ints, sems):
    n_src, aux_blk, lanes = moved.shape
    n_orb = ints_any.shape[2]
    n_zl = parts.shape[2]
    n_cyc = n_src // n_zl
    shift, core = place[0], place[2]
    loads = []
    per = aux_blk // N_LOAD
    for n in range(N_LOAD):
        part = pl.ds(n * per, per)
        for src, dst in ((ints_any, ints), (other_any, other_ints)):
            loads.append(pltpu.make_async_copy(src.at[part], dst.at[part], sems.at[len(loads)]))
            loads[-1].start()
    wide[...] = moved[...].reshape(n_src * aux_blk, lanes).astype(F32)
    for p in range(0, aux_blk, 2):
        if p % per == 0:
            loads[p // per * 2].wait()
            loads[p // per * 2 + 1].wait()
        left, right = [], []
        for q in (p, p + 1):
            x = wide[pl.ds(q, n_src, stride=aux_blk), :]
            left.append(pltpu.roll(x, core * (lanes // 2), 1).astype(BF16))
            right += [ints[q], other_ints[q]]
        term = dot(jnp.concatenate(left, axis=1), jnp.concatenate(right, axis=0), 1, 0)
        if p == 0:
            acc[...] = term
        else:
            acc[...] += term
    for k in range(n_cyc):
        target = lax.rem(k + shift, n_cyc)
        zh = lax.rem(lax.div(target, N_Y), 2)
        xy = lax.div(target, 2 * N_Y) * N_Y + lax.rem(target, N_Y)
        for g in range(n_orb // lanes):
            parts[xy * 2 + g % 2, zh, g // 2] = acc[k * n_zl : (k + 1) * n_zl, g * lanes : (g + 1) * lanes]


def join_kernel(lag, keep, recv, out):
    n_dest, n_zh, n_zl = lag.shape[:3]
    pieces = [lag[:, a, b] for a in range(n_zh) for b in range(n_zl)]
    n_lag = n_zh * n_zl * lag.shape[3]
    aux_blk, lanes = keep.shape[2:]
    n_low = keep.shape[1] // 2
    out[:, :n_lag] = jnp.concatenate(pieces, axis=1).astype(BF16)
    for xy in range(n_dest // 2):
        for low in range(n_low):
            for c in range(2):
                g = 2 * low + c
                out[2 * xy + c, n_lag + low * aux_blk : n_lag + (low + 1) * aux_blk] = (
                    keep[xy, g] + recv[xy, g].astype(F32)
                ).astype(BF16)


def plane_kernel(got, out):
    n_src = got.shape[0]
    n_z, n_rows, lanes = out.shape
    n_zl = n_z // 2
    n_lag = n_z * n_zl
    aux_blk = n_rows - 2 * n_zl
    n_low = (got.shape[1] - n_lag) // aux_blk
    for c in range(2):
        total = got[c, :n_lag].astype(F32)
        for src in range(c + 2, n_src, 2):
            total = total + got[src, :n_lag].astype(F32)
        for z in range(n_z):
            out[z, c * n_zl : (c + 1) * n_zl] = total[z * n_zl : (z + 1) * n_zl]
        for yl in range(2):
            first = 2 * yl + c
            total = got[first, n_lag:].astype(F32)
            for src in range(first + 4, n_src, 4):
                total = total + got[src, n_lag:].astype(F32)
            for low in range(n_low):
                z = c * n_zl + n_low * yl + low
                out[z, 2 * n_zl :] = total[low * aux_blk : (low + 1) * aux_blk]


def last_kernel(got, aux, lag):
    total = jnp.sum(got[...], axis=0)
    n_zl = lag.shape[0] // 2
    aux[...] = total[2 * n_zl :, : aux.shape[1]]
    for z in range(n_zl):
        for c in range(2):
            lag[2 * z + c : 2 * z + c + 1] = total[c * n_zl + z : c * n_zl + z + 1]


def local(b_factors, occ_energy, vir_energy, integrals, window_start):
    n_cyc = lax.axis_size(CYC)
    n_zl = lax.axis_size("zl")
    n_grp = n_zl * 2
    yl = lax.axis_index("yl")
    core = lax.axis_index("core")
    cyc = lax.axis_index(CYC)
    grp = lax.axis_index("zl") * 2 + core
    own = b_factors[0]
    n_vir, n_aux = own.shape
    n_orb = integrals.shape[2]
    aux_blk = n_aux // n_cyc
    shift = jnp.mod(window_start[0] + 1, n_cyc)
    place = jnp.stack([shift, yl, core]).astype(jnp.int32)

    mate = swap_yl(own)

    ints = jnp.transpose(integrals, (1, 0, 2))
    ints, other_ints, mate = lax.optimization_barrier((ints, swap_cores(ints), mate))

    sub = n_vir // n_cyc
    spread = exchange_all(own.reshape(n_cyc, sub, n_aux), CYC)
    turned = call(
        turn_kernel,
        jax.ShapeDtypeStruct((n_cyc, 2, sub, n_aux), BF16),
        [],
        0,
        8 * n_vir * n_aux,
        place,
        spread,
        specs=[smem, vmem],
    )
    rows = exchange_all(turned, CYC)

    step = 1 - 2 * yl
    energy_i = occ_energy[jnp.mod(cyc + shift, n_cyc) * n_grp + grp]
    energy_j = occ_energy[jnp.mod(cyc + jnp.stack([0, step, -step]), n_cyc) * n_grp + grp]
    dens = call(
        pair_kernel,
        jax.ShapeDtypeStruct((n_cyc, n_vir // LANES, aux_blk, LANES), BF16),
        [],
        18 * n_vir * n_vir * n_aux,
        5 * 2 * n_vir * n_aux,
        energy_i + energy_j,
        vir_energy[None, :],
        vir_energy[:, None],
        rows,
        own,
        mate,
        specs=[smem] + [vmem] * 5,
    )
    moved = exchange_all(dens.reshape(n_cyc * n_zl, aux_blk, LANES), CYC + ("zl",))

    n_xy = n_cyc // 2
    near, far = call(
        aux_kernel,
        (
            jax.ShapeDtypeStruct((n_xy, n_grp, aux_blk, LANES), F32),
            jax.ShapeDtypeStruct((n_xy, n_grp, aux_blk, LANES), BF16),
        ),
        [pltpu.VMEM((n_aux, n_grp * LANES), F32)],
        2 * n_vir * n_aux * n_aux,
        10 * n_vir * n_aux,
        place,
        dens,
        rows,
        specs=[smem, vmem, vmem],
    )
    keep, send = call(
        fold_kernel,
        (
            jax.ShapeDtypeStruct((n_xy, n_grp // 2, aux_blk, LANES), F32),
            jax.ShapeDtypeStruct((n_xy, n_grp // 2, aux_blk, LANES), BF16),
        ),
        [],
        0,
        9 * n_vir * n_aux,
        place,
        near,
        swap_cores(far),
        specs=[smem, vmem, vmem],
    )
    recv = swap_yl(send)

    lag = call(
        lag_kernel,
        jax.ShapeDtypeStruct((n_cyc, 2, n_zl, n_zl, LANES), F32),
        [
            pltpu.VMEM((n_vir * n_aux // LANES, LANES), F32),
            pltpu.VMEM((n_cyc * n_zl, n_orb), F32),
            pltpu.VMEM(ints.shape, BF16),
            pltpu.VMEM(ints.shape, BF16),
            pltpu.SemaphoreType.DMA((2 * N_LOAD,)),
        ],
        2 * n_vir * n_aux * n_orb,
        2 * n_vir * n_aux * 10,
        place,
        moved,
        ints,
        other_ints,
        specs=[smem, vmem, hbm, hbm],
    )
    n_rows = 2 * n_zl * n_zl + n_zl // 2 * aux_blk
    parts = call(
        join_kernel,
        jax.ShapeDtypeStruct((n_cyc, n_rows, LANES), BF16),
        [],
        0,
        8 * n_cyc * n_rows * LANES,
        lag,
        keep,
        recv,
        specs=[vmem] * 3,
    )
    plane = call(
        plane_kernel,
        jax.ShapeDtypeStruct((2 * n_zl, n_grp + aux_blk, LANES), F32),
        [],
        n_cyc * n_rows * LANES,
        2 * n_cyc * n_rows * LANES,
        exchange_all(parts, PLANE),
        specs=[vmem],
    )
    aux_metric, lagrangian = call(
        last_kernel,
        (jax.ShapeDtypeStruct((aux_blk, n_aux // n_grp), F32), jax.ShapeDtypeStruct((n_grp, LANES), F32)),
        [],
        0,
        4 * 2 * n_zl * 32 * LANES,
        exchange_all(plane, DEPTH),
        specs=[vmem],
    )
    return (aux_metric, lagrangian)


def solution(mesh):
    n_occ, n_grp = mesh.shape["occ"], mesh.shape["grp"]
    sizes = (n_occ // (2 * N_Y), 2, N_Y // 2, 2, n_grp // 2, 2)
    fine = Mesh(mesh.devices.reshape(sizes), CYC + ("zl", "core"))
    grp = ("zl", "core")
    placed = (P(CYC + grp, None, None), P(), P(), P(grp, CYC, None), P())
    return jax.shard_map(
        local,
        mesh=fine,
        in_specs=placed,
        out_specs=(P(CYC, grp), P(CYC, grp)),
        check_vma=False,
    )
```
